512 devices in a mesh: seq: 128 (over z_hi, y, x, core), mp: 4 (over z_lo).
Axes of the slice: x: 4, y: 8, z: 8 (z_hi: 2, z_lo: 4; z = z_hi * 4 + z_lo), core: 2. Of those that a mesh axis runs over, the one named last changes fastest.
Arguments:
- coarse: bfloat16 [768, 16384], P('mp', 'seq'), may hold values from -6 to 6
- skip: bfloat16 [768, 32768], P('mp', 'seq'), may hold values from -6 to 6
- conv_weight: bfloat16 [3, 768, 768], P(None, 'mp'), may hold values from -0.125 to 0.125
- conv_bias: float32 [768], P('mp'), may hold values from -3 to 3
- head_weight: bfloat16 [768, 512], P(None, 'mp'), may hold values from -0.21875 to 0.21875
- head_bias: float32 [512], P('mp'), may hold values from -3 to 3
- counts: int32 [32768, 512], P('seq', 'mp'), may hold values from 0 to 3
- seg_mask: int32 [16, 512], P(None, 'mp'), may hold values 0 or 1
Outputs:
- grad_skip: bfloat16 [768, 32768], P('mp', 'seq')
- grad_coarse: bfloat16 [768, 16384], P('mp', 'seq')
- grad_head: float32 [768, 512], P('seq', 'mp')
- grad_conv: float32 [768, 3, 768], P('seq', None, 'mp')
The draws below stay inside these ranges and needn't reach their ends.
All inputs are finite; a program needn't handle non-finite values. No bound on the sum of `seg_mask` on one device may be relied on, other than what follows from the above.
Results may differ from the reference program's by a relative error of at most 0.0068.
Values may be sent and summed in bfloat16 or wider, within the bound.
A program may use at most 64 MiB of HBM per device.

```python
import jax
import jax.numpy as jnp
from jax import lax

C = 768
TRACKS = 512
KERNEL = 3
TOKENS = 32768
SEG = 2048
NSEG = 16


def place_ends(drawn, rng, smallest, high):
    index_at = [jax.random.randint(jax.random.fold_in(rng, axis), (), 0, length) for axis, length in enumerate(drawn.shape)]
    longest = drawn.shape.index(max(drawn.shape))
    beside = index_at[:longest] + [(index_at[longest] + 1) % drawn.shape[longest]] + index_at[longest + 1:]
    return drawn.at[tuple(index_at)].set(smallest).at[tuple(beside)].set(high)


def steps_of(rng, shape, split, smallest, largest):
    level = 1.0
    for axis_at, blocks in split:
        steps = jax.random.uniform(jax.random.fold_in(jax.random.fold_in(rng, 6), axis_at), (blocks,), jnp.float32, smallest / len(split), largest / len(split))
        level = level * jnp.repeat(jnp.exp(steps), shape[axis_at] // blocks).reshape((-1,) + (1,) * (len(shape) - 1 - axis_at))
    return level


def scatter_about(key, shape, spread, limit, cuts=(), kind=jnp.bfloat16):
    factor_of = steps_of(key, shape, cuts, -0.22, 0.18) if cuts else 1.0
    entries = jax.random.normal(key, shape, jnp.float32) * spread * factor_of
    return jnp.minimum(jnp.maximum(entries, -limit), limit).astype(kind)


def setup_inputs(seed: int = 0) -> dict:
    arg_keys = jax.random.split(jax.random.key(seed), 9)
    coarse = scatter_about(arg_keys[0], (C, TOKENS // 2), 1.0, 6.0, ((0, 4), (1, 128)))
    skip = scatter_about(arg_keys[1], (C, TOKENS), 1.0, 6.0, ((0, 4), (1, 128)))
    conv_weight = scatter_about(arg_keys[2], (KERNEL, C, C), (KERNEL * C) ** -0.5, 0.125, ((1, 4),))
    conv_bias = scatter_about(arg_keys[3], (C,), 0.5, 3.0, ((0, 4),), jnp.float32)
    head_weight = scatter_about(arg_keys[4], (C, TRACKS), C ** -0.5, 0.21875, ((1, 4),))
    head_bias = scatter_about(arg_keys[5], (TRACKS,), 0.5, 3.0, ((0, 4),), jnp.float32)
    counts = place_ends(jax.random.randint(arg_keys[6], (TOKENS, TRACKS), 0, 4), jax.random.fold_in(arg_keys[6], 1), 0, 3).astype(jnp.int32)
    seg_mask = place_ends((jax.random.randint(arg_keys[7], (NSEG, TRACKS), 0, 4) < 3).astype(jnp.int32), jax.random.fold_in(arg_keys[7], 1), 0, 1)
    return {"coarse": coarse, "skip": skip, "conv_weight": conv_weight, "conv_bias": conv_bias, "head_weight": head_weight, "head_bias": head_bias, "counts": counts, "seg_mask": seg_mask}


root_two_pi = 0.7978845608028654
cubic_coef = 0.044715

def gelu_value(inputs):
    inner = root_two_pi * (inputs + cubic_coef * inputs * inputs * inputs)
    return 0.5 * inputs * (1.0 + jnp.tanh(inner))

def gelu_slope(inputs):
    inner = root_two_pi * (inputs + cubic_coef * inputs * inputs * inputs)
    tangent = jnp.tanh(inner)
    return 0.5 * (1.0 + tangent) + 0.5 * inputs * (1.0 - tangent * tangent) * root_two_pi * (1.0 + 3.0 * cubic_coef * inputs * inputs)

def reference(coarse, skip, conv_weight, conv_bias, head_weight, head_bias, counts, seg_mask):
    length = skip.shape[1]
    taps = conv_weight.shape[0]
    reach = taps // 2
    tracks_all = head_weight.shape[1]
    doubled = jnp.repeat(coarse.T.astype(jnp.float32), 2, axis=0)
    summed = (doubled + skip.T.astype(jnp.float32)).astype(jnp.bfloat16)
    padded = jnp.pad(summed, ((reach, reach), (0, 0)))
    conv_out = jnp.zeros((length, conv_weight.shape[1]), jnp.float32)
    for offset in range(taps):
        conv_out = conv_out + jnp.dot(padded[offset:offset + length], conv_weight[offset].T, preferred_element_type=jnp.float32)
    before = conv_out + conv_bias
    hidden = (summed.astype(jnp.float32) + gelu_value(before)).astype(jnp.bfloat16)
    logits = jnp.dot(hidden, head_weight, preferred_element_type=jnp.float32) + head_bias
    predicted = jax.nn.softplus(logits) + 0.5
    observed = counts.astype(jnp.float32)
    segments = length // SEG
    pred_total = lax.optimization_barrier(jnp.sum(predicted.reshape(segments, SEG, tracks_all), axis=1))
    count_total = lax.optimization_barrier(jnp.sum(observed.reshape(segments, SEG, tracks_all), axis=1))
    mask_float = seg_mask.astype(jnp.float32)
    ratio = (mask_float * 4.0 * count_total / pred_total)[:, None, :]
    mask_wide = mask_float[:, None, :]
    slope_pred = mask_wide * (1.0 - 5.0 * observed.reshape(segments, SEG, tracks_all) / predicted.reshape(segments, SEG, tracks_all)) + ratio
    slope_pred = slope_pred.reshape(length, tracks_all)
    grad_logits = (slope_pred * jax.nn.sigmoid(logits)).astype(jnp.bfloat16)
    grad_hidden = jnp.dot(grad_logits, head_weight.T, preferred_element_type=jnp.float32)
    scale_back = 1.0 / jnp.sqrt(jnp.float32(length))
    grad_head = jnp.dot(hidden.T, grad_logits, preferred_element_type=jnp.float32) * scale_back
    grad_before = (grad_hidden * gelu_slope(before)).astype(jnp.bfloat16)
    grad_padded = jnp.pad(grad_before, ((reach, reach), (0, 0)))
    back = jnp.zeros((length, conv_weight.shape[2]), jnp.float32)
    for offset in range(taps):
        start_row = 2 * reach - offset
        back = back + jnp.dot(grad_padded[start_row:start_row + length], conv_weight[offset], preferred_element_type=jnp.float32)
    grad_input = grad_hidden + back
    grad_skip = grad_input.astype(jnp.bfloat16)
    grad_coarse = lax.optimization_barrier(jnp.sum(grad_input.reshape(length // 2, 2, grad_input.shape[1]), axis=1)).astype(jnp.bfloat16)
    pieces = []
    for offset in range(taps):
        pieces.append(jnp.dot(padded[offset:offset + length].T, grad_before, preferred_element_type=jnp.float32))
    grad_conv = jnp.stack(pieces, axis=1) * scale_back
    return (grad_skip.T, grad_coarse.T, grad_head, grad_conv)
```

```python
import functools
import math

import jax
import jax.numpy as jnp
from jax import lax
from jax.experimental import pallas as pl
from jax.experimental.pallas import tpu as pltpu
from jax.sharding import PartitionSpec as P

root_two_pi = 0.7978845608028654
cubic_coef = 0.044715
multi_weight = 5.0
pseudo_count = 0.5

CORES, XS, YS, HIS, MPS = 2, 4, 8, 2, 4
ROW = XS * CORES
SEQ = HIS * YS * ROW

F32 = jnp.float32
BF16 = jnp.bfloat16


def gelu_parts(v):
    tangent = jnp.tanh(root_two_pi * (v + cubic_coef * v * v * v))
    value = 0.5 * v * (1.0 + tangent)
    slope = 0.5 * (1.0 + tangent) + 0.5 * v * (1.0 - tangent * tangent) * root_two_pi * (
        1.0 + 3.0 * cubic_coef * v * v
    )
    return value, slope


def dot(left, right, dims):
    return lax.dot_general(left, right, (dims, ((), ())), preferred_element_type=F32)


NN = ((1,), (0,))
NT = ((1,), (1,))
TN = ((0,), (0,))


def iota(shape, axis):
    return lax.broadcasted_iota(jnp.int32, shape, axis)


def one_hot(mask):
    return jnp.where(mask, 1.0, 0.0).astype(BF16)


def body(
    coarse, skip, weight, conv_bias, head, head_bias, counts, seg_mask,
    out_skip, out_coarse, out_head, out_conv,
    summed_all, edge_in, edge_all, hidden_all, head_own, track_all, seg_all,
    before_ref, slope_ref, grad_hidden_ref, gb_ref, gedge, shifted,
    pick, summed_pick, hidden_pick, turned,
    back_send, back_recv, own_half, core_send, core_recv,
    x_send, x_recv, y_send, y_recv, hi_send, hi_recv,
    edge_sems, sum_sems, rows_sems, hid_sems, head_sems, seg_sems, track_sems,
    gedge_sems, back_sems, core_sems, x_sems, y_sems, hi_sems,
):
    width, length = skip.shape
    half = length // 2
    channels = head.shape[0]
    tracks = head.shape[1]
    unit = channels // SEQ
    cols = core_send.shape[1]
    conv_cols = 3 * width
    scale_back = 1.0 / math.sqrt(length * SEQ)

    s = lax.axis_index("seq")
    z = lax.axis_index("mp")
    core = lax.rem(s, CORES)
    x = lax.rem(s // CORES, XS)
    y = lax.rem(s // ROW, YS)
    hi = s // (ROW * YS)

    mp_peer = [lax.rem(z + d, MPS) for d in range(MPS)]
    row_base = s - lax.rem(s, ROW)
    row_peer = [row_base + lax.rem(lax.rem(s, ROW) + d, ROW) for d in range(ROW)]
    core_peer = s + 1 - 2 * core
    x_peer = [s + CORES * (lax.rem(x + d, XS) - x) for d in range(XS)]
    y_peer = [s + ROW * (lax.rem(y + d, YS) - y) for d in range(YS)]
    hi_peer = s + ROW * YS * (1 - 2 * hi)
    right = lax.rem(s + 1, SEQ)
    left = lax.rem(s + SEQ - 1, SEQ)

    def send(src, dst, sems, slot, device):
        copy = pltpu.make_async_remote_copy(
            src_ref=src,
            dst_ref=dst,
            send_sem=sems.at[0, slot],
            recv_sem=sems.at[1, slot],
            device_id=device,
            device_id_type=pl.DeviceIdType.MESH,
        )
        copy.start()
        return copy

    barrier = pltpu.get_barrier_semaphore()
    greeted = [{"mp": p} for p in mp_peer[1:]]
    greeted += [{"seq": p} for p in row_peer[1:] + y_peer[1:] + [hi_peer, left, right]]
    for device in greeted:
        pl.semaphore_signal(barrier, inc=1, device_id=device, device_id_type=pl.DeviceIdType.MESH)

    spread = one_hot(iota((half, length), 1) // 2 == iota((half, length), 0))
    doubled = dot(coarse[...], spread, NN)
    summed = (doubled + skip[...].astype(F32)).astype(BF16)
    summed_all[z] = summed

    pl.semaphore_wait(barrier, len(greeted))

    edge_copies = [
        send(summed_all.at[z, :, pl.ds(half, half)], edge_in.at[0], edge_sems, 0, {"seq": right}),
        send(summed_all.at[z, :, pl.ds(0, half)], edge_in.at[1], edge_sems, 1, {"seq": left}),
    ]
    sum_copies = [
        send(summed_all.at[z], summed_all.at[z], sum_sems, d - 1, {"mp": mp_peer[d]})
        for d in range(1, MPS)
    ]

    group = channels // ROW
    row = iota((group, channels), 0)
    lane = iota((group, channels), 1)
    step = HIS * unit
    y_step = jnp.zeros_like(row)
    for j in range(1, YS):
        y_step = y_step + jnp.where(row >= step * j, 1, 0)
    rest = row - step * y_step
    hi_step = jnp.where(rest >= unit, 1, 0)
    rest = rest - unit * hi_step
    y_at = y + y_step
    y_at = jnp.where(y_at >= YS, y_at - YS, y_at)
    hi_at = jnp.where(hi_step == 1, 1 - hi, hi)
    base = ((hi_at * YS + y_at) * ROW) * unit + rest
    for c in range(CORES):
        core_at = core if c == 0 else 1 - core
        for d in range(XS):
            x_at = lax.rem(x + d, XS)
            place = (c * XS + d) * group
            pick[place : place + group, :] = one_hot(
                lane == base + (x_at * CORES + core_at) * unit
            )

    for k in range(3):
        turned[k] = weight[k].T

    for copy in edge_copies:
        copy.wait()
    first = jnp.where(s == 0, 0.0, 1.0).astype(BF16)
    last = jnp.where(s == SEQ - 1, 0.0, 1.0).astype(BF16)
    shape = (16, half)
    low_row = one_hot((iota(shape, 0) == 0) & (iota(shape, 1) == half - 1)) * first
    high_row = one_hot((iota(shape, 0) == 1) & (iota(shape, 1) == 0)) * last
    rows = dot(low_row, edge_in[0], NT) + dot(high_row, edge_in[1], NT)
    edge_all[z] = jnp.zeros((16, edge_all.shape[2]), BF16)
    edge_all[z, :, 0:width] = rows.astype(BF16)
    rows_copies = [
        send(edge_all.at[z], edge_all.at[z], rows_sems, d - 1, {"mp": mp_peer[d]})
        for d in range(1, MPS)
    ]

    for copy in sum_copies:
        copy.wait()
    head_copies = [
        send(
            head.at[pl.ds(pl.multiple_of(mp_peer[d] * width, width), width), :],
            head_own.at[z],
            head_sems,
            d - 1,
            {"mp": mp_peer[d]},
        )
        for d in range(1, MPS)
    ]
    head_own[z] = head[pl.ds(pl.multiple_of(z * width, width), width), :]
    summed_full = summed_all[...].reshape(channels, length)
    bias_rows = jnp.zeros((16, width), F32)
    bias = conv_bias[...]
    part0 = bias.astype(BF16).astype(F32)
    part1 = (bias - part0).astype(BF16).astype(F32)
    part2 = bias - part0 - part1
    at = iota((16, width), 0)
    bias_rows = jnp.where(at == 0, part0, jnp.where(at == 1, part1, jnp.where(at == 2, part2, 0.0)))
    before = dot(bias_rows.astype(BF16), jnp.ones((16, length), BF16), TN)
    before = before + dot(weight[1], summed_full, NN)
    from_low = dot(weight[0], summed_full, NN)
    from_high = dot(weight[2], summed_full, NN)

    for copy in rows_copies:
        copy.wait()
    edges = jnp.zeros((16, channels), F32)
    span = edge_all.shape[2]
    for k in range(MPS):
        placed = one_hot(
            (iota((span, channels), 1) == iota((span, channels), 0) + k * width)
            & (iota((span, channels), 0) < width)
        )
        edges = edges + dot(edge_all[k], placed, NN)
    edges = edges.astype(BF16)
    low_col = dot(weight[0], edges, NT)[:, 0:1]
    high_col = dot(weight[2], edges, NT)[:, 1:2]
    lanes = iota((width, length), 1)
    before = before + jnp.where(lanes == 0, low_col, pltpu.roll(from_low, 1, 1))
    before = before + jnp.where(lanes == length - 1, high_col, pltpu.roll(from_high, length - 1, 1))
    value, slope = gelu_parts(before)
    hidden_all[z] = (summed_all[z].astype(F32) + value).astype(BF16)
    hidden_copies = [
        send(hidden_all.at[z], hidden_all.at[z], hid_sems, d - 1, {"mp": mp_peer[d]})
        for d in range(1, MPS)
    ]
    slope_ref[...] = slope
    summed_pick[...] = dot(pick[...], summed_full, NN).astype(BF16)
    observed = counts[...].astype(F32)
    mine = lax.rem(s, ROW)
    seg_all[mine] = jnp.zeros(seg_all.shape[1:], F32)
    seg_all[mine, 1:2, :] = jnp.sum(observed, axis=0, keepdims=True)

    for copy in hidden_copies:
        copy.wait()
    hidden_full = hidden_all[...].reshape(channels, length)
    logits = dot(hidden_full, head[...], TN) + head_bias[...]
    small = jnp.exp(-jnp.abs(logits))
    predicted = jnp.maximum(logits, 0.0) + jnp.log1p(small) + pseudo_count
    seg_all[mine, 0:1, :] = jnp.sum(predicted, axis=0, keepdims=True)
    seg_copies = [
        send(seg_all.at[mine], seg_all.at[mine], seg_sems, d - 1, {"seq": row_peer[d]})
        for d in range(1, ROW)
    ]
    hidden_pick[...] = dot(pick[...], hidden_full, NN).astype(BF16)
    sigmoid = jnp.where(logits >= 0.0, 1.0, small) / (1.0 + small)
    ratio = multi_weight * observed / predicted
    mask_row = seg_mask[pl.ds(s // ROW, 1), :].astype(F32)
    for copy in seg_copies:
        copy.wait()
    totals = seg_all[0]
    for k in range(1, ROW):
        totals = totals + seg_all[k]
    share = 1.0 + (multi_weight - 1.0) * totals[1:2, :] / totals[0:1, :]
    grad_logits = (mask_row * (share - ratio) * sigmoid).astype(BF16)
    track_all[z] = grad_logits
    track_copies = [
        send(track_all.at[z], track_all.at[z], track_sems, d - 1, {"mp": mp_peer[d]})
        for d in range(1, MPS)
    ]
    grad_head = dot(hidden_pick[...], grad_logits, NN)
    own_half[:, cols - tracks : cols] = grad_head[: channels // 2]
    core_send[:, cols - tracks : cols] = grad_head[channels // 2 :].astype(BF16)

    for copy in head_copies:
        copy.wait()
    for copy in track_copies:
        copy.wait()
    grad_hidden = dot(head_own[0], track_all[0], NT)
    for k in range(1, MPS):
        grad_hidden = grad_hidden + dot(head_own[k], track_all[k], NT)
    gb = (grad_hidden * slope_ref[...]).astype(BF16)
    gb_ref[...] = gb
    gedge_copies = [
        send(gb_ref.at[:, pl.ds(half, half)], gedge.at[0], gedge_sems, 0, {"seq": right}),
        send(gb_ref.at[:, pl.ds(0, half)], gedge.at[1], gedge_sems, 1, {"seq": left}),
    ]
    grad_hidden_ref[...] = grad_hidden
    shifted[width : 2 * width, :] = gb
    gb_wide = gb.astype(F32)
    to_left = pltpu.roll(gb_wide, length - 1, 1)
    to_right = pltpu.roll(gb_wide, 1, 1)
    for copy in gedge_copies:
        copy.wait()
    keep_low = jnp.where(s == 0, 0.0, 1.0)
    keep_high = jnp.where(s == SEQ - 1, 0.0, 1.0)
    low_col = gedge[0].astype(F32)[:, half - 1 : half] * keep_low
    high_col = gedge[1].astype(F32)[:, 0:1] * keep_high
    shifted[0:width, :] = jnp.where(lanes == length - 1, high_col, to_left).astype(BF16)
    shifted[2 * width :, :] = jnp.where(lanes == 0, low_col, to_right).astype(BF16)

    for k in range(ROW // 2, ROW):
        part = dot(summed_pick[k * group : (k + 1) * group, :], shifted[...], NT)
        at = (k - ROW // 2) * group
        core_send[at : at + group, 0:conv_cols] = part.astype(BF16)
        core_send[at : at + group, conv_cols : cols - tracks] = jnp.zeros(
            (group, cols - tracks - conv_cols), BF16
        )
    core_copy = send(core_send, core_recv, core_sems, 0, {"seq": core_peer})

    for d in (2, 1, 3, 0):
        at = pl.ds(pl.multiple_of(mp_peer[d] * width, width), width)
        total = jnp.zeros((width, length), F32)
        for k in range(3):
            total = total + dot(turned[k, at, :], shifted[k * width : (k + 1) * width, :], NN)
        if d == 0:
            grad_hidden_ref[...] += total
        else:
            back_send[d - 1] = total.astype(BF16)
    back_copies = [
        send(back_send.at[d - 1], back_recv.at[d - 1], back_sems, d - 1, {"mp": mp_peer[d]})
        for d in range(1, MPS)
    ]

    for k in range(ROW // 2):
        part = dot(summed_pick[k * group : (k + 1) * group, :], shifted[...], NT)
        at = k * group
        own_half[at : at + group, 0:conv_cols] = part
        own_half[at : at + group, conv_cols : cols - tracks] = jnp.zeros(
            (group, cols - tracks - conv_cols), F32
        )
    core_copy.wait()
    for d in range(1, XS):
        at = d * group
        x_send[d - 1] = (
            own_half[at : at + group, :] + core_recv[at : at + group, :].astype(F32)
        ).astype(BF16)
    x_copies = [
        send(x_send.at[d - 1], x_recv.at[d - 1], x_sems, d - 1, {"seq": x_peer[d]})
        for d in range(1, XS)
    ]
    total = own_half[0:group, :] + core_recv[0:group, :].astype(F32)
    for copy in x_copies:
        copy.wait()
    for d in range(1, XS):
        total = total + x_recv[d - 1].astype(F32)
    own_half[0:group, :] = total
    for d in range(1, YS):
        y_send[d - 1, 0:step, :] = own_half[d * step : (d + 1) * step, :].astype(BF16)
        y_send[d - 1, step:16, :] = jnp.zeros((16 - step, cols), BF16)
    y_copies = [
        send(y_send.at[d - 1], y_recv.at[d - 1], y_sems, d - 1, {"seq": y_peer[d]})
        for d in range(1, YS)
    ]

    for copy in back_copies:
        copy.wait()
    total = grad_hidden_ref[...]
    for d in range(1, MPS):
        total = total + back_recv[d - 1].astype(F32)
    out_skip[...] = total.astype(BF16)
    high = total.astype(BF16)
    rest = total - high.astype(F32)
    mid = rest.astype(BF16)
    low = (rest - mid.astype(F32)).astype(BF16)
    pairs = dot(high, spread, NT) + dot(mid, spread, NT) + dot(low, spread, NT)
    out_coarse[...] = pairs.astype(BF16)

    for copy in y_copies:
        copy.wait()
    total = own_half[0:16, :]
    for d in range(1, YS):
        total = total + y_recv[d - 1].astype(F32)
    hi_send[...] = total.astype(BF16)
    hi_copy = send(hi_send, hi_recv, hi_sems, 0, {"seq": hi_peer})
    hi_copy.wait()
    final = (total[0:unit, :] + hi_recv[...].astype(F32)[unit : 2 * unit, :]) * scale_back
    out_head[...] = final[:, cols - tracks :]
    for k in range(3):
        out_conv[:, k, :] = final[:, k * width : (k + 1) * width]


def shards(coarse, skip, conv_weight, conv_bias, head_weight, head_bias, counts, seg_mask):
    width, length = skip.shape
    channels, tracks = head_weight.shape
    half = length // 2
    group = channels // ROW
    cols = -(-3 * width // 128) * 128 + tracks
    unit = channels // SEQ
    wide = -(-width // 128) * 128

    def sems(count):
        return pltpu.SemaphoreType.DMA((2, count))

    scratch = [
        pltpu.VMEM((MPS, width, length), BF16),
        pltpu.VMEM((2, width, half), BF16),
        pltpu.VMEM((MPS, 16, wide), BF16),
        pltpu.VMEM((MPS, width, length), BF16),
        pltpu.VMEM((MPS, width, tracks), BF16),
        pltpu.VMEM((MPS, length, tracks), BF16),
        pltpu.VMEM((ROW, 8, tracks), F32),
        pltpu.VMEM((width, length), F32),
        pltpu.VMEM((width, length), F32),
        pltpu.VMEM((width, length), F32),
        pltpu.VMEM((width, length), BF16),
        pltpu.VMEM((2, width, half), BF16),
        pltpu.VMEM((3 * width, length), BF16),
        pltpu.VMEM((channels, channels), BF16),
        pltpu.VMEM((channels, length), BF16),
        pltpu.VMEM((channels, length), BF16),
        pltpu.VMEM((3, channels, width), BF16),
        pltpu.VMEM((MPS - 1, width, length), BF16),
        pltpu.VMEM((MPS - 1, width, length), BF16),
        pltpu.VMEM((channels // 2, cols), F32),
        pltpu.VMEM((channels // 2, cols), BF16),
        pltpu.VMEM((channels // 2, cols), BF16),
        pltpu.VMEM((XS - 1, group, cols), BF16),
        pltpu.VMEM((XS - 1, group, cols), BF16),
        pltpu.VMEM((YS - 1, 16, cols), BF16),
        pltpu.VMEM((YS - 1, 16, cols), BF16),
        pltpu.VMEM((16, cols), BF16),
        pltpu.VMEM((16, cols), BF16),
        sems(2), sems(MPS - 1), sems(MPS - 1), sems(MPS - 1), sems(MPS - 1), sems(ROW - 1),
        sems(MPS - 1), sems(2), sems(MPS - 1), sems(1), sems(XS - 1), sems(YS - 1), sems(1),
    ]
    vmem = pl.BlockSpec(memory_space=pltpu.VMEM)
    return pl.pallas_call(
        body,
        out_shape=(
            jax.ShapeDtypeStruct((width, length), BF16),
            jax.ShapeDtypeStruct((width, half), BF16),
            jax.ShapeDtypeStruct((unit, tracks), F32),
            jax.ShapeDtypeStruct((unit, 3, width), F32),
        ),
        in_specs=[vmem] * 8,
        out_specs=(vmem,) * 4,
        scratch_shapes=scratch,
        compiler_params=pltpu.CompilerParams(
            collective_id=0, has_side_effects=True, vmem_limit_bytes=48 * 1024 * 1024
        ),
    )(
        coarse, skip, conv_weight, conv_bias.reshape(1, -1), head_weight,
        head_bias.reshape(1, -1), counts, seg_mask,
    )


def solution(mesh):
    in_specs = (
        P("mp", "seq"),
        P("mp", "seq"),
        P(None, "mp", None),
        P("mp"),
        P(None, "mp"),
        P("mp"),
        P("seq", "mp"),
        P(None, "mp"),
    )
    out_specs = (P("mp", "seq"), P("mp", "seq"), P("seq", "mp"), P("seq", None, "mp"))
    return jax.shard_map(shards, mesh=mesh, in_specs=in_specs, out_specs=out_specs, check_vma=False)
```

```python
import functools
import math

import jax
import jax.numpy as jnp
from jax import lax
from jax.experimental import pallas as pl
from jax.experimental.pallas import tpu as pltpu
from jax.sharding import PartitionSpec as P

root_two_pi = 0.7978845608028654
cubic_coef = 0.044715
multi_weight = 5.0
pseudo_count = 0.5

CORES, XS, YS, HIS, MPS = 2, 4, 8, 2, 4
ROW = XS * CORES
FAR = YS * HIS
SEQ = FAR * ROW

F32 = jnp.float32
BF16 = jnp.bfloat16
VMEM_BYTES = 63 * 1024 * 1024
MESH = pl.DeviceIdType.MESH


def gelu_parts(v):
    tangent = jnp.tanh(root_two_pi * (v + cubic_coef * v * v * v))
    value = 0.5 * v * (1.0 + tangent)
    slope = 0.5 * (1.0 + tangent) + 0.5 * v * (1.0 - tangent * tangent) * root_two_pi * (
        1.0 + 3.0 * cubic_coef * v * v
    )
    return value, slope


def dot(left, right, dims):
    return lax.dot_general(left, right, (dims, ((), ())), preferred_element_type=F32)


NN = ((1,), (0,))
NT = ((1,), (1,))
TN = ((0,), (0,))


def iota(shape, axis):
    return lax.broadcasted_iota(jnp.int32, shape, axis)


def one_hot(mask):
    return jnp.where(mask, 1.0, 0.0).astype(BF16)


def body(
    coarse_in, skip_in, weight_in, conv_bias_in, head_in, head_bias_in, counts_in, seg_mask_in,
    out_skip, out_coarse, out_head, out_conv,
    coarse, skip, weight, conv_bias, head, head_bias, counts, seg_mask,
    summed_all, edge_own, edge_all, hidden_all, head_own, track_all, seg_all,
    slope_ref, grad_hidden_ref, gb_ref, gedge, shifted,
    pick, summed_pick, hidden_pick, turned,
    back_send, back_recv,
    top_own, top_core_send, top_core_recv, top_x_send, top_x_recv, top_far_send, top_far_recv,
    own_half, core_send, core_recv, x_send, x_recv, far_own, far_send, far_recv,
    res_skip, res_coarse, res_head, res_conv,
    in_sems, out_sems, edge_sems, sum_sems, hid_sems, head_sems, seg_sems, track_sems,
    gedge_sems, back_sems, top_core_sems, top_x_sems, top_far_sems, core_sems, x_sems, far_sems,
):
    width, length = skip.shape
    half = length // 2
    channels = head.shape[0]
    tracks = head.shape[1]
    unit = channels // SEQ
    group = channels // ROW
    cols = core_send.shape[1]
    conv_cols = 3 * width
    scale_back = 1.0 / math.sqrt(length * SEQ)

    s = lax.axis_index("seq")
    z = lax.axis_index("mp")
    core = lax.rem(s, CORES)
    x = lax.rem(s // CORES, XS)
    y = lax.rem(s // ROW, YS)
    hi = s // (ROW * YS)
    mine = lax.rem(s, ROW)

    mp_peer = [lax.rem(z + d, MPS) for d in range(MPS)]
    row_peer = [s - mine + lax.rem(mine + d, ROW) for d in range(ROW)]
    core_peer = s + 1 - 2 * core
    x_peer = [s + CORES * (lax.rem(x + d, XS) - x) for d in range(XS)]
    far_peer = [
        s + ROW * (lax.rem(y + p // HIS, YS) - y) + ROW * YS * (lax.rem(hi + p % HIS, HIS) - hi)
        for p in range(FAR)
    ]
    right = lax.rem(s + 1, SEQ)
    left = lax.rem(s + SEQ - 1, SEQ)

    def send(src, dst, sems, slot, device):
        copy = pltpu.make_async_remote_copy(
            src_ref=src,
            dst_ref=dst,
            send_sem=sems.at[0, slot],
            recv_sem=sems.at[1, slot],
            device_id=device,
            device_id_type=MESH,
        )
        copy.start()
        return copy

    def store(src, dst, slot):
        copy = pltpu.make_async_copy(src, dst, out_sems.at[slot])
        copy.start()
        return copy

    def wait(copies):
        for copy in copies:
            copy.wait()

    barrier = pltpu.get_barrier_semaphore()
    greeted = [{"mp": p} for p in mp_peer[1:]]
    greeted += [{"seq": p, "mp": q} for p in (left, right) for q in mp_peer]
    greeted += [{"seq": p} for p in row_peer[1:] + far_peer[1:]]
    for device in greeted:
        pl.semaphore_signal(barrier, inc=1, device_id=device, device_id_type=MESH)

    loads = []
    for slot, (src, dst) in enumerate(
        (
            (coarse_in, coarse), (skip_in, skip), (weight_in, weight), (conv_bias_in, conv_bias),
            (head_in, head), (head_bias_in, head_bias), (counts_in, counts),
            (seg_mask_in, seg_mask),
        )
    ):
        copy = pltpu.make_async_copy(src, dst, in_sems.at[slot])
        copy.start()
        loads.append(copy)

    spread = one_hot(iota((half, length), 1) // 2 == iota((half, length), 0))
    edge_own[...] = jnp.zeros(edge_own.shape, BF16)
    wait(loads[:2])
    doubled = dot(coarse[...], spread, NN)
    summed = (doubled + skip[...].astype(F32)).astype(BF16)
    summed_all[z] = summed
    ends = one_hot(
        ((iota((16, length), 0) == 0) & (iota((16, length), 1) == 0))
        | ((iota((16, length), 0) == 1) & (iota((16, length), 1) == length - 1))
    )
    edge_own[:, 0:width] = dot(ends, summed, NT).astype(BF16)

    pl.semaphore_wait(barrier, len(greeted))

    edge_copies = []
    for side, neighbour in ((0, right), (1, left)):
        for d in range(MPS):
            edge_copies.append(
                send(
                    edge_own, edge_all.at[side, z], edge_sems, side * MPS + d,
                    {"seq": neighbour, "mp": mp_peer[d]},
                )
            )
    sum_copies = [
        send(summed_all.at[z], summed_all.at[z], sum_sems, d - 1, {"mp": mp_peer[d]})
        for d in range(1, MPS)
    ]

    row = iota((group, channels), 0)
    lane = iota((group, channels), 1)
    step = HIS * unit
    y_step = jnp.zeros_like(row)
    for j in range(1, YS):
        y_step = y_step + jnp.where(row >= step * j, 1, 0)
    rest = row - step * y_step
    hi_step = jnp.where(rest >= unit, 1, 0)
    rest = rest - unit * hi_step
    y_at = y + y_step
    y_at = jnp.where(y_at >= YS, y_at - YS, y_at)
    hi_at = jnp.where(hi_step == 1, 1 - hi, hi)
    base = ((hi_at * YS + y_at) * ROW) * unit + rest
    for c in range(CORES):
        core_at = core if c == 0 else 1 - core
        for d in range(XS):
            x_at = lax.rem(x + d, XS)
            place = (c * XS + d) * group
            pick[place : place + group, :] = one_hot(
                lane == base + (x_at * CORES + core_at) * unit
            )

    wait(loads[2:])
    for k in range(3):
        turned[k] = weight[k].T
    bias = conv_bias[...]
    part0 = bias.astype(BF16).astype(F32)
    part1 = (bias - part0).astype(BF16).astype(F32)
    part2 = bias - part0 - part1
    at = iota((16, width), 0)
    bias_rows = jnp.where(at == 0, part0, jnp.where(at == 1, part1, jnp.where(at == 2, part2, 0.0)))
    head_own[z] = head[pl.ds(pl.multiple_of(z * width, width), width), :]
    observed = counts[...].astype(F32)
    seg_all[mine] = jnp.zeros(seg_all.shape[1:], F32)
    seg_all[mine, 1:2, :] = jnp.sum(observed, axis=0, keepdims=True)
    far_own[...] = jnp.zeros(far_own.shape, F32)
    top_far_send[...] = jnp.zeros(top_far_send.shape, BF16)
    own_half[:, conv_cols:] = jnp.zeros((channels // 2, cols - conv_cols), F32)
    core_send[:, conv_cols:] = jnp.zeros((channels // 2, cols - conv_cols), BF16)

    wait(edge_copies)
    span = edge_all.shape[3]
    low_rows = jnp.zeros((16, channels), F32)
    high_rows = jnp.zeros((16, channels), F32)
    for k in range(MPS):
        placed = one_hot(
            (iota((span, channels), 1) == iota((span, channels), 0) + k * width)
            & (iota((span, channels), 0) < width)
        )
        low_rows = low_rows + dot(edge_all[0, k], placed, NN)
        high_rows = high_rows + dot(edge_all[1, k], placed, NN)
    keep_low = jnp.where(s == 0, 0.0, 1.0)
    keep_high = jnp.where(s == SEQ - 1, 0.0, 1.0)
    low_rows = (low_rows * keep_low).astype(BF16)
    high_rows = (high_rows * keep_high).astype(BF16)
    before = dot(bias_rows.astype(BF16), jnp.ones((16, length), BF16), TN)
    lanes = iota((width, length), 1)
    before = before + jnp.where(lanes == 0, dot(weight[0], low_rows, NT)[:, 1:2], 0.0)
    before = before + jnp.where(
        lanes == length - 1, dot(weight[2], high_rows, NT)[:, 0:1], 0.0
    )

    wait(sum_copies)
    summed_full = summed_all[...].reshape(channels, length)
    before = before + dot(weight[1], summed_full, NN)
    from_low = dot(weight[0], summed_full, NN)
    from_high = dot(weight[2], summed_full, NN)
    before = before + jnp.where(lanes == 0, 0.0, pltpu.roll(from_low, 1, 1))
    before = before + jnp.where(lanes == length - 1, 0.0, pltpu.roll(from_high, length - 1, 1))
    value, slope = gelu_parts(before)
    hidden_all[z] = (summed_all[z].astype(F32) + value).astype(BF16)
    hidden_copies = [
        send(hidden_all.at[z], hidden_all.at[z], hid_sems, d - 1, {"mp": mp_peer[d]})
        for d in range(1, MPS)
    ]
    slope_ref[...] = slope
    lanes_group = iota((group, length), 1)
    for k in range(ROW):
        at = slice(k * group, (k + 1) * group)
        picked = dot(pick[at, :], summed_full, NN)
        low_col = dot(pick[at, :], low_rows, NT)[:, 1:2]
        high_col = dot(pick[at, :], high_rows, NT)[:, 0:1]
        summed_pick[0, at, :] = jnp.where(
            lanes_group == 0, low_col, pltpu.roll(picked, 1, 1)
        ).astype(BF16)
        summed_pick[1, at, :] = picked.astype(BF16)
        summed_pick[2, at, :] = jnp.where(
            lanes_group == length - 1, high_col, pltpu.roll(picked, length - 1, 1)
        ).astype(BF16)

    wait(hidden_copies)
    hidden_full = hidden_all[...].reshape(channels, length)
    logits = dot(hidden_full, head[...], TN) + head_bias[...]
    small = jnp.exp(-jnp.abs(logits))
    predicted = jnp.maximum(logits, 0.0) + jnp.log1p(small) + pseudo_count
    seg_all[mine, 0:1, :] = jnp.sum(predicted, axis=0, keepdims=True)
    seg_copies = [
        send(seg_all.at[mine], seg_all.at[mine], seg_sems, d - 1, {"seq": row_peer[d]})
        for d in range(1, ROW)
    ]
    head_copies = [
        send(
            head.at[pl.ds(pl.multiple_of(mp_peer[d] * width, width), width), :],
            head_own.at[z],
            head_sems,
            d - 1,
            {"mp": mp_peer[d]},
        )
        for d in range(1, MPS)
    ]
    hidden_pick[...] = dot(pick[...], hidden_full, NN).astype(BF16)
    sigmoid = jnp.where(logits >= 0.0, 1.0, small) / (1.0 + small)
    ratio = multi_weight * observed / predicted
    mask_row = seg_mask[pl.ds(s // ROW, 1), :].astype(F32)
    wait(seg_copies)
    totals = seg_all[0]
    for k in range(1, ROW):
        totals = totals + seg_all[k]
    share = 1.0 + (multi_weight - 1.0) * totals[1:2, :] / totals[0:1, :]
    grad_logits = (mask_row * (share - ratio) * sigmoid).astype(BF16)
    track_all[z] = grad_logits
    track_copies = [
        send(track_all.at[z], track_all.at[z], track_sems, d - 1, {"mp": mp_peer[d]})
        for d in range(1, MPS)
    ]
    top_core_send[...] = dot(hidden_pick[channels // 2 :, :], grad_logits, NN).astype(BF16)
    top_core_copy = send(top_core_send, top_core_recv, top_core_sems, 0, {"seq": core_peer})
    top_own[...] = dot(hidden_pick[: channels // 2, :], grad_logits, NN)
    wait([top_core_copy])
    for d in range(1, XS):
        at = slice(d * group, (d + 1) * group)
        top_x_send[d - 1] = (top_own[at, :] + top_core_recv[at, :].astype(F32)).astype(BF16)
    top_x_copies = [
        send(top_x_send.at[d - 1], top_x_recv.at[d - 1], top_x_sems, d - 1, {"seq": x_peer[d]})
        for d in range(1, XS)
    ]

    wait(head_copies)
    wait(track_copies)
    grad_hidden = dot(head_own[0], track_all[0], NT)
    for k in range(1, MPS):
        grad_hidden = grad_hidden + dot(head_own[k], track_all[k], NT)
    gb = (grad_hidden * slope_ref[...]).astype(BF16)
    gb_ref[...] = gb
    gedge_copies = [
        send(gb_ref.at[:, pl.ds(half, half)], gedge.at[0], gedge_sems, 0, {"seq": right}),
        send(gb_ref.at[:, pl.ds(0, half)], gedge.at[1], gedge_sems, 1, {"seq": left}),
    ]

    for k in range(ROW // 2, ROW):
        at = slice((k - ROW // 2) * group, (k - ROW // 2 + 1) * group)
        for tap in range(3):
            part = dot(summed_pick[tap, k * group : (k + 1) * group, :], gb, NT)
            core_send[at, tap * width : (tap + 1) * width] = part.astype(BF16)
    core_copy = send(core_send, core_recv, core_sems, 0, {"seq": core_peer})
    grad_hidden_ref[...] = grad_hidden
    for k in range(ROW // 2):
        at = slice(k * group, (k + 1) * group)
        for tap in range(3):
            part = dot(summed_pick[tap, at, :], gb, NT)
            own_half[at, tap * width : (tap + 1) * width] = part
    wait([core_copy])
    for d in range(1, XS):
        at = slice(d * group, (d + 1) * group)
        x_send[d - 1] = (own_half[at, :] + core_recv[at, :].astype(F32)).astype(BF16)
    x_copies = [
        send(x_send.at[d - 1], x_recv.at[d - 1], x_sems, d - 1, {"seq": x_peer[d]})
        for d in range(1, XS)
    ]
    own_half[0:group, :] += core_recv[0:group, :].astype(F32)

    wait(top_x_copies)
    total = top_own[0:group, :] + top_core_recv[0:group, :].astype(F32)
    for d in range(1, XS):
        total = total + top_x_recv[d - 1].astype(F32)
    top_own[0:group, :] = total
    for p in range(1, FAR):
        top_far_send[p - 1, 0:unit, :] = top_own[p * unit : (p + 1) * unit, :].astype(BF16)
    top_far_copies = [
        send(
            top_far_send.at[p - 1], top_far_recv.at[p - 1], top_far_sems, p - 1,
            {"seq": far_peer[p]},
        )
        for p in range(1, FAR)
    ]

    gb_wide = gb_ref[...].astype(F32)
    to_left = pltpu.roll(gb_wide, length - 1, 1)
    to_right = pltpu.roll(gb_wide, 1, 1)
    shifted[width : 2 * width, :] = gb_ref[...]
    wait(gedge_copies)
    low_col = gedge[0].astype(F32)[:, half - 1 : half] * keep_low
    high_col = gedge[1].astype(F32)[:, 0:1] * keep_high
    shifted[0:width, :] = jnp.where(lanes == length - 1, high_col, to_left).astype(BF16)
    shifted[2 * width :, :] = jnp.where(lanes == 0, low_col, to_right).astype(BF16)
    back_copies = []
    for d in (1, 2, 3, 0):
        at = pl.ds(pl.multiple_of(mp_peer[d] * width, width), width)
        total = jnp.zeros((width, length), F32)
        for k in range(3):
            total = total + dot(turned[k, at, :], shifted[k * width : (k + 1) * width, :], NN)
        if d == 0:
            grad_hidden_ref[...] += total
        else:
            back_send[d - 1] = total.astype(BF16)
            back_copies.append(
                send(back_send.at[d - 1], back_recv.at[d - 1], back_sems, d - 1, {"mp": mp_peer[d]})
            )

    wait(x_copies)
    total = own_half[0:group, :]
    for d in range(1, XS):
        total = total + x_recv[d - 1].astype(F32)
    own_half[0:group, :] = total
    tiles = cols // 128
    far_copies = []
    for p in list(range(1, FAR)) + [0]:
        for j in range(tiles):
            far_own[p, j * unit : (j + 1) * unit, :] = own_half[
                p * unit : (p + 1) * unit, j * 128 : (j + 1) * 128
            ]
        if p > 0:
            far_send[p - 1] = far_own[p].astype(BF16)
            far_copies.append(
                send(far_send.at[p - 1], far_recv.at[p - 1], far_sems, p - 1, {"seq": far_peer[p]})
            )

    wait(back_copies)
    total = grad_hidden_ref[...]
    for d in range(1, MPS):
        total = total + back_recv[d - 1].astype(F32)
    res_skip[...] = total.astype(BF16)
    stores = [store(res_skip, out_skip, 0)]
    high = total.astype(BF16)
    rest = total - high.astype(F32)
    mid = rest.astype(BF16)
    low = (rest - mid.astype(F32)).astype(BF16)
    pairs = dot(high, spread, NT) + dot(mid, spread, NT) + dot(low, spread, NT)
    res_coarse[...] = pairs.astype(BF16)
    stores.append(store(res_coarse, out_coarse, 1))

    wait(top_far_copies)
    total = top_own[0:16, :]
    for p in range(1, FAR):
        total = total + top_far_recv[p - 1].astype(F32)
    res_head[...] = total[0:unit, :] * scale_back
    stores.append(store(res_head, out_head, 2))

    wait(far_copies)
    total = far_own[0]
    for p in range(1, FAR):
        total = total + far_recv[p - 1].astype(F32)
    total = total * scale_back
    final = jnp.concatenate([total[j * unit : (j + 1) * unit, :] for j in range(tiles)], axis=1)
    for k in range(3):
        res_conv[:, k, :] = final[:, k * width : (k + 1) * width]
    stores.append(store(res_conv, out_conv, 3))
    wait(stores)


def write_out(*refs):
    count = len(refs) // 2
    sems = refs[-1]
    copies = [
        pltpu.make_async_copy(refs[k], refs[count + k], sems.at[k]) for k in range(count)
    ]
    for copy in copies:
        copy.start()
    for copy in copies:
        copy.wait()


def shards(coarse, skip, conv_weight, conv_bias, head_weight, head_bias, counts, seg_mask):
    width, length = skip.shape
    channels, tracks = head_weight.shape
    half = length // 2
    group = channels // ROW
    cols = -(-3 * width // 128) * 128
    unit = channels // SEQ
    wide = -(-width // 128) * 128
    packed = -(-unit * (cols // 128) // 16) * 16

    args = (
        coarse, skip, conv_weight, conv_bias.reshape(1, -1), head_weight,
        head_bias.reshape(1, -1), counts, seg_mask,
    )

    shapes = (
        jax.ShapeDtypeStruct((width, length), BF16),
        jax.ShapeDtypeStruct((width, half), BF16),
        jax.ShapeDtypeStruct((unit, tracks), F32),
        jax.ShapeDtypeStruct((unit, 3, width), F32),
    )

    def sems(count):
        return pltpu.SemaphoreType.DMA((2, count))

    scratch = [pltpu.VMEM(a.shape, a.dtype) for a in args]
    scratch += [
        pltpu.VMEM((MPS, width, length), BF16),
        pltpu.VMEM((16, wide), BF16),
        pltpu.VMEM((2, MPS, 16, wide), BF16),
        pltpu.VMEM((MPS, width, length), BF16),
        pltpu.VMEM((MPS, width, tracks), BF16),
        pltpu.VMEM((MPS, length, tracks), BF16),
        pltpu.VMEM((ROW, 8, tracks), F32),
        pltpu.VMEM((width, length), F32),
        pltpu.VMEM((width, length), F32),
        pltpu.VMEM((width, length), BF16),
        pltpu.VMEM((2, width, half), BF16),
        pltpu.VMEM((3 * width, length), BF16),
        pltpu.VMEM((channels, channels), BF16),
        pltpu.VMEM((3, channels, length), BF16),
        pltpu.VMEM((channels, length), BF16),
        pltpu.VMEM((3, channels, width), BF16),
        pltpu.VMEM((MPS - 1, width, length), BF16),
        pltpu.VMEM((MPS - 1, width, length), BF16),
        pltpu.VMEM((channels // 2, tracks), F32),
        pltpu.VMEM((channels // 2, tracks), BF16),
        pltpu.VMEM((channels // 2, tracks), BF16),
        pltpu.VMEM((XS - 1, group, tracks), BF16),
        pltpu.VMEM((XS - 1, group, tracks), BF16),
        pltpu.VMEM((FAR - 1, 16, tracks), BF16),
        pltpu.VMEM((FAR - 1, 16, tracks), BF16),
        pltpu.VMEM((channels // 2, cols), F32),
        pltpu.VMEM((channels // 2, cols), BF16),
        pltpu.VMEM((channels // 2, cols), BF16),
        pltpu.VMEM((XS - 1, group, cols), BF16),
        pltpu.VMEM((XS - 1, group, cols), BF16),
        pltpu.VMEM((FAR, packed, 128), F32),
        pltpu.VMEM((FAR - 1, packed, 128), BF16),
        pltpu.VMEM((FAR - 1, packed, 128), BF16),
        *(pltpu.VMEM(a.shape, a.dtype) for a in shapes),
        pltpu.SemaphoreType.DMA((len(args),)),
        pltpu.SemaphoreType.DMA((len(shapes),)),
        sems(2 * MPS), sems(MPS - 1), sems(MPS - 1), sems(MPS - 1), sems(ROW - 1),
        sems(MPS - 1), sems(2), sems(MPS - 1), sems(1), sems(XS - 1), sems(FAR - 1),
        sems(1), sems(XS - 1), sems(FAR - 1),
    ]
    hbm = pl.BlockSpec(memory_space=pltpu.HBM)
    results = pl.pallas_call(
        body,
        out_shape=shapes,
        in_specs=[hbm] * len(args),
        out_specs=(hbm,) * len(shapes),
        scratch_shapes=scratch,
        compiler_params=pltpu.CompilerParams(
            collective_id=0, has_side_effects=True, vmem_limit_bytes=VMEM_BYTES
        ),
    )(*args)
    return pl.pallas_call(
        write_out,
        out_shape=shapes,
        in_specs=[hbm] * len(shapes),
        out_specs=(hbm,) * len(shapes),
        scratch_shapes=[pltpu.SemaphoreType.DMA((len(shapes),))],
        compiler_params=pltpu.CompilerParams(vmem_limit_bytes=VMEM_BYTES),
    )(*results)


def solution(mesh):
    in_specs = (
        P("mp", "seq"),
        P("mp", "seq"),
        P(None, "mp", None),
        P("mp"),
        P(None, "mp"),
        P("mp"),
        P("seq", "mp"),
        P(None, "mp"),
    )
    out_specs = (P("mp", "seq"), P("mp", "seq"), P("seq", "mp"), P("seq", None, "mp"))
    return jax.shard_map(shards, mesh=mesh, in_specs=in_specs, out_specs=out_specs, check_vma=False)
```

```python
import functools
import math

import jax
import jax.numpy as jnp
from jax import lax
from jax.experimental import pallas as pl
from jax.experimental.pallas import tpu as pltpu
from jax.sharding import PartitionSpec as P

root_two_pi = 0.7978845608028654
cubic_coef = 0.044715
multi_weight = 5.0
pseudo_count = 0.5

CORES, XS, YS, HIS, MPS = 2, 4, 8, 2, 4
ROW = XS * CORES
FAR = YS * HIS
SEQ = FAR * ROW

F32 = jnp.float32
BF16 = jnp.bfloat16
VMEM_BYTES = 63 * 1024 * 1024
MESH = pl.DeviceIdType.MESH


def gelu_parts(v):
    tangent = jnp.tanh(root_two_pi * (v + cubic_coef * v * v * v))
    value = 0.5 * v * (1.0 + tangent)
    slope = 0.5 * (1.0 + tangent) + 0.5 * v * (1.0 - tangent * tangent) * root_two_pi * (
        1.0 + 3.0 * cubic_coef * v * v
    )
    return value, slope


def dot(left, right, dims):
    return lax.dot_general(left, right, (dims, ((), ())), preferred_element_type=F32)


NN = ((1,), (0,))
NT = ((1,), (1,))
TN = ((0,), (0,))


def iota(shape, axis):
    return lax.broadcasted_iota(jnp.int32, shape, axis)


def one_hot(mask):
    return jnp.where(mask, 1.0, 0.0).astype(BF16)


def body(
    coarse_in, skip_in, weight_in, conv_bias_in, head_in, head_bias_in, counts_in, seg_mask_in,
    out_skip, out_coarse, out_head, out_conv,
    coarse, skip, weight, conv_bias, head_bias, counts, seg_mask,
    summed_all, edge_own, edge_all, mid_all, hidden_all, head_wide, counts_all, count_all,
    small_all, seg_all, slope_ref, grad_hidden_ref, gb_ref, gedge, shifted,
    pick, summed_pick, hidden_pick, turned,
    back_send, back_recv,
    top_own, top_core_send, top_core_recv, top_x_send, top_x_recv, top_far_send, top_far_recv,
    a_own, a_core_send, a_core_recv, a_x_send, a_x_recv, a_far_own, a_far_send, a_far_recv,
    b_own, b_core_send, b_core_recv, b_x_send, b_x_recv, b_far_own, b_far_send, b_far_recv,
    res_skip, res_coarse, res_head, res_conv,
    in_sems, out_sems, edge_sems, mid_sems, sum_sems, hid_sems, head_sems, spread_sems,
    counts_sems, count_sems, small_sems, seg_sems,
    gedge_sems, back_sems, top_core_sems, top_x_sems, top_far_sems,
    a_core_sems, a_x_sems, a_far_sems, b_core_sems, b_x_sems, b_far_sems,
):
    width, length = skip.shape
    half = length // 2
    channels = head_in.shape[0]
    tracks = head_in.shape[1]
    unit = channels // SEQ
    group = channels // ROW
    scale_back = 1.0 / math.sqrt(length * SEQ)

    s = lax.axis_index("seq")
    z = lax.axis_index("mp")
    core = lax.rem(s, CORES)
    x = lax.rem(s // CORES, XS)
    y = lax.rem(s // ROW, YS)
    hi = s // (ROW * YS)
    mine = lax.rem(s, ROW)

    mp_peer = [lax.rem(z + d, MPS) for d in range(MPS)]
    row_peer = [s - mine + lax.rem(mine + d, ROW) for d in range(ROW)]
    core_peer = s + 1 - 2 * core
    x_peer = [s + CORES * (lax.rem(x + d, XS) - x) for d in range(XS)]
    far_peer = [
        s + ROW * (lax.rem(y + p // HIS, YS) - y) + ROW * YS * (lax.rem(hi + p % HIS, HIS) - hi)
        for p in range(FAR)
    ]
    right = lax.rem(s + 1, SEQ)
    left = lax.rem(s + SEQ - 1, SEQ)

    def send(src, dst, sems, slot, device):
        copy = pltpu.make_async_remote_copy(
            src_ref=src,
            dst_ref=dst,
            send_sem=sems.at[0, slot],
            recv_sem=sems.at[1, slot],
            device_id=device,
            device_id_type=MESH,
        )
        copy.start()
        return copy

    def store(src, dst, slot):
        copy = pltpu.make_async_copy(src, dst, out_sems.at[slot])
        copy.start()
        return copy

    def wait(copies):
        for copy in copies:
            copy.wait()

    barrier = pltpu.get_barrier_semaphore()
    greeted = [{"mp": p} for p in mp_peer[1:]]
    greeted += [{"seq": p, "mp": q} for p in (left, right) for q in mp_peer]
    greeted += [{"seq": p} for p in row_peer[1:] + far_peer[1:]]
    for device in greeted:
        pl.semaphore_signal(barrier, inc=1, device_id=device, device_id_type=MESH)

    loads = []
    for slot, (src, dst) in enumerate(
        (
            (coarse_in, coarse), (skip_in, skip), (head_in, head_wide.at[:, pl.ds(0, tracks)]),
            (counts_in, counts), (weight_in, weight), (conv_bias_in, conv_bias),
            (head_bias_in, head_bias), (seg_mask_in, seg_mask),
        )
    ):
        copy = pltpu.make_async_copy(src, dst, in_sems.at[slot])
        copy.start()
        loads.append(copy)

    spread = one_hot(iota((half, length), 1) // 2 == iota((half, length), 0))
    edge_own[...] = jnp.zeros(edge_own.shape, BF16)
    wait(loads[:2])
    doubled = dot(coarse[...], spread, NN)
    summed = (doubled + skip[...].astype(F32)).astype(BF16)
    summed_all[z] = summed
    shape = (16, length)
    at_row, at_lane = iota(shape, 0), iota(shape, 1)
    ends = one_hot(
        ((at_row == 0) & (at_lane == 0))
        | ((at_row == 1) & (at_lane == length - 1))
        | ((at_row == 2) & (at_lane == half))
    )
    edge_own[:, 0:width] = dot(ends, summed, NT).astype(BF16)
    mid_all[z] = edge_own[...]
    pl.semaphore_wait(barrier, len(greeted))

    lower, upper = pl.ds(0, half), pl.ds(half, half)
    edge_copies = []
    for side, neighbour in ((0, right), (1, left)):
        for d in range(MPS):
            edge_copies.append(
                send(
                    edge_own, edge_all.at[side, z], edge_sems, side * MPS + d,
                    {"seq": neighbour, "mp": mp_peer[d]},
                )
            )
    mid_copies = [
        send(edge_own, mid_all.at[z], mid_sems, d - 1, {"mp": mp_peer[d]}) for d in range(1, MPS)
    ]

    def gather(ref, lanes, sems, first):
        return [
            send(
                ref.at[z, :, lanes], ref.at[z, :, lanes], sems, first + d - 1, {"mp": mp_peer[d]}
            )
            for d in range(1, MPS)
        ]

    sum_low = gather(summed_all, lower, sum_sems, 0)
    wait(loads[2:3])
    my_rows = pl.ds(pl.multiple_of(mine * group, group), group)
    head_copies = [
        send(
            head_wide.at[my_rows, pl.ds(0, tracks)],
            head_wide.at[my_rows, pl.ds((MPS - d) * tracks, tracks)],
            head_sems,
            d - 1,
            {"mp": mp_peer[d]},
        )
        for d in range(1, MPS)
    ]
    sum_high = gather(summed_all, upper, sum_sems, MPS - 1)
    wait(loads[3:])
    observed = counts[...].astype(F32)
    counts_all[0] = observed.astype(BF16)
    count_all[mine] = jnp.zeros(count_all.shape[1:], F32)
    count_all[mine, 0:1, :] = jnp.sum(observed, axis=0, keepdims=True)
    count_copies = [
        send(count_all.at[mine], count_all.at[mine], count_sems, d - 1, {"seq": row_peer[d]})
        for d in range(1, ROW)
    ]

    row = iota((group, channels), 0)
    lane = iota((group, channels), 1)
    step = HIS * unit
    y_step = jnp.zeros_like(row)
    for j in range(1, YS):
        y_step = y_step + jnp.where(row >= step * j, 1, 0)
    rest = row - step * y_step
    hi_step = jnp.where(rest >= unit, 1, 0)
    rest = rest - unit * hi_step
    y_at = y + y_step
    y_at = jnp.where(y_at >= YS, y_at - YS, y_at)
    hi_at = jnp.where(hi_step == 1, 1 - hi, hi)
    base = ((hi_at * YS + y_at) * ROW) * unit + rest
    for c in range(CORES):
        core_at = core if c == 0 else 1 - core
        for d in range(XS):
            x_at = lax.rem(x + d, XS)
            place = (c * XS + d) * group
            pick[place : place + group, :] = one_hot(
                lane == base + (x_at * CORES + core_at) * unit
            )

    for k in range(3):
        turned[k] = weight[k].T
    bias = conv_bias[...]
    part0 = bias.astype(BF16).astype(F32)
    part1 = (bias - part0).astype(BF16).astype(F32)
    part2 = bias - part0 - part1
    at = iota((16, width), 0)
    bias_rows = jnp.where(at == 0, part0, jnp.where(at == 1, part1, jnp.where(at == 2, part2, 0.0)))
    bias_wide = dot(bias_rows.astype(BF16), jnp.ones((16, half), BF16), TN)
    a_far_own[...] = jnp.zeros(a_far_own.shape, F32)
    b_far_own[...] = jnp.zeros(b_far_own.shape, F32)
    top_far_send[...] = jnp.zeros(top_far_send.shape, BF16)
    b_cols = b_own.shape[1]
    b_own[:, width:] = jnp.zeros((channels // 2, b_cols - width), F32)
    b_core_send[:, width:] = jnp.zeros((channels // 2, b_cols - width), BF16)

    wait(edge_copies)
    wait(mid_copies)
    span = edge_all.shape[3]
    low_rows = jnp.zeros((16, channels), F32)
    high_rows = jnp.zeros((16, channels), F32)
    mid_rows = jnp.zeros((16, channels), F32)
    for k in range(MPS):
        placed = one_hot(
            (iota((span, channels), 1) == iota((span, channels), 0) + k * width)
            & (iota((span, channels), 0) < width)
        )
        low_rows = low_rows + dot(edge_all[0, k], placed, NN)
        high_rows = high_rows + dot(edge_all[1, k], placed, NN)
        mid_rows = mid_rows + dot(mid_all[k], placed, NN)
    keep_low = jnp.where(s == 0, 0.0, 1.0)
    keep_high = jnp.where(s == SEQ - 1, 0.0, 1.0)
    low_rows = (low_rows * keep_low).astype(BF16)
    high_rows = (high_rows * keep_high).astype(BF16)
    mid_rows = mid_rows.astype(BF16)
    low_col = dot(weight[0], low_rows, NT)[:, 1:2]
    mid_col = dot(weight[2], mid_rows, NT)[:, 2:3]
    high_col = dot(weight[2], high_rows, NT)[:, 0:1]
    lanes = iota((width, half), 1)

    def convolve(at, first_col, last_col):
        block = summed_all[:, :, at].reshape(channels, half)
        from_low = dot(weight[0], block, NN)
        from_high = dot(weight[2], block, NN)
        before = bias_wide + dot(weight[1], block, NN)
        before = before + jnp.where(lanes == 0, first_col, pltpu.roll(from_low, 1, 1))
        before = before + jnp.where(
            lanes == half - 1, last_col, pltpu.roll(from_high, half - 1, 1)
        )
        value, slope = gelu_parts(before)
        hidden_all[z, :, at] = (summed_all[z, :, at].astype(F32) + value).astype(BF16)
        slope_ref[:, at] = slope
        return from_low[:, half - 1 : half]

    wait(sum_low)
    next_col = convolve(slice(0, half), low_col, mid_col)
    hidden_low = gather(hidden_all, lower, hid_sems, 0)

    wait(head_copies)
    spread_copies = [
        send(
            head_wide.at[my_rows, pl.ds(tracks, (MPS - 1) * tracks)],
            head_wide.at[my_rows, pl.ds(tracks, (MPS - 1) * tracks)],
            spread_sems,
            d - 1,
            {"seq": row_peer[d]},
        )
        for d in range(1, ROW)
    ]

    wait(sum_high)
    convolve(slice(half, length), next_col, high_col)
    hidden_high = gather(hidden_all, upper, hid_sems, MPS - 1)

    wait(count_copies)
    counted = count_all[0]
    for k in range(1, ROW):
        counted = counted + count_all[k]
    small_all[0] = jnp.zeros(small_all.shape[1:], F32)
    small_all[0, 0:1, :] = head_bias[...]
    small_all[0, 1:2, :] = seg_mask[pl.ds(s // ROW, 1), :].astype(F32)
    small_all[0, 2:3, :] = counted[0:1, :]
    small_copies = [
        send(small_all.at[0], small_all.at[MPS - d], small_sems, d - 1, {"mp": mp_peer[d]})
        for d in range(1, MPS)
    ]

    summed_full = summed_all[...].reshape(channels, length)
    lanes_group = iota((group, length), 1)
    for k in range(ROW):
        at = slice(k * group, (k + 1) * group)
        picked = dot(pick[at, :], summed_full, NN)
        low_edge = dot(pick[at, :], low_rows, NT)[:, 1:2]
        high_edge = dot(pick[at, :], high_rows, NT)[:, 0:1]
        summed_pick[0, at, :] = jnp.where(
            lanes_group == 0, low_edge, pltpu.roll(picked, 1, 1)
        ).astype(BF16)
        summed_pick[1, at, :] = picked.astype(BF16)
        summed_pick[2, at, :] = jnp.where(
            lanes_group == length - 1, high_edge, pltpu.roll(picked, length - 1, 1)
        ).astype(BF16)

    wait(hidden_low)
    counts_copies = [
        send(counts_all.at[0], counts_all.at[MPS - d], counts_sems, d - 1, {"mp": mp_peer[d]})
        for d in range(1, MPS)
    ]
    wait(small_copies)
    wait(spread_copies)
    wait(hidden_high)
    hidden_full = hidden_all[...].reshape(channels, length)
    products = dot(hidden_full, head_wide[...], TN)
    sigmoids, inverses = [], []
    seg_all[mine] = jnp.zeros(seg_all.shape[1:], F32)
    for d in range(MPS):
        logits = products[:, d * tracks : (d + 1) * tracks] + small_all[d, 0:1, :]
        small = jnp.exp(-jnp.abs(logits))
        predicted = jnp.maximum(logits, 0.0) + jnp.log1p(small) + pseudo_count
        seg_all[mine, d : d + 1, :] = jnp.sum(predicted, axis=0, keepdims=True)
        sigmoids.append((logits, small))
        inverses.append(predicted)
    seg_copies = [
        send(seg_all.at[mine], seg_all.at[mine], seg_sems, d - 1, {"seq": row_peer[d]})
        for d in range(1, ROW)
    ]
    for d in range(MPS):
        logits, small = sigmoids[d]
        sigmoids[d] = small_all[d, 1:2, :] * jnp.where(logits >= 0.0, 1.0, small) / (1.0 + small)
        inverses[d] = multi_weight / inverses[d]
    hidden_pick[...] = dot(pick[...], hidden_full, NN).astype(BF16)
    wait(counts_copies)
    wait(seg_copies)
    totals = seg_all[0]
    for k in range(1, ROW):
        totals = totals + seg_all[k]
    blocks = []
    for d in range(MPS):
        share = 1.0 + (multi_weight - 1.0) * small_all[d, 2:3, :] / totals[d : d + 1, :]
        blocks.append(
            ((share - counts_all[d].astype(F32) * inverses[d]) * sigmoids[d]).astype(BF16)
        )
    grad_logits = blocks[0]
    own_rows = pl.ds(pl.multiple_of(z * width, width), width)
    grad_hidden = dot(head_wide[own_rows, :], jnp.concatenate(blocks, axis=1), NT)
    gb = (grad_hidden * slope_ref[...]).astype(BF16)
    gb_ref[...] = gb

    class Sums:
        def __init__(self, refs, sems):
            self.own, self.core_send, self.core_recv, self.x_send, self.x_recv = refs[:5]
            self.far_own, self.far_send, self.far_recv = refs[5:]
            self.core_sems, self.x_sems, self.far_sems = sems

        def to_core(self):
            self.core_copy = send(
                self.core_send, self.core_recv, self.core_sems, 0, {"seq": core_peer}
            )

        def to_x(self):
            self.core_copy.wait()
            self.x_copies = []
            for d in range(1, XS):
                at = slice(d * group, (d + 1) * group)
                self.x_send[d - 1] = (
                    self.own[at, :] + self.core_recv[at, :].astype(F32)
                ).astype(BF16)
                self.x_copies.append(
                    send(
                        self.x_send.at[d - 1], self.x_recv.at[d - 1], self.x_sems, d - 1,
                        {"seq": x_peer[d]},
                    )
                )
            self.own[0:group, :] += self.core_recv[0:group, :].astype(F32)

        def add_x(self):
            wait(self.x_copies)
            total = self.own[0:group, :]
            for d in range(1, XS):
                total = total + self.x_recv[d - 1].astype(F32)
            self.own[0:group, :] = total

        def to_far(self):
            self.add_x()
            self.far_copies = []
            for p in list(range(1, FAR)) + [0]:
                for j in range(self.own.shape[1] // 128):
                    self.far_own[p, j * unit : (j + 1) * unit, :] = self.own[
                        p * unit : (p + 1) * unit, j * 128 : (j + 1) * 128
                    ]
                if p > 0:
                    self.far_send[p - 1] = self.far_own[p].astype(BF16)
                    self.far_copies.append(
                        send(
                            self.far_send.at[p - 1], self.far_recv.at[p - 1], self.far_sems,
                            p - 1, {"seq": far_peer[p]},
                        )
                    )

        def end(self):
            wait(self.far_copies)
            total = self.far_own[0]
            for p in range(1, FAR):
                total = total + self.far_recv[p - 1].astype(F32)
            total = total * scale_back
            return jnp.concatenate(
                [total[j * unit : (j + 1) * unit, :] for j in range(self.own.shape[1] // 128)],
                axis=1,
            )

    sums_a = Sums(
        (a_own, a_core_send, a_core_recv, a_x_send, a_x_recv, a_far_own, a_far_send, a_far_recv),
        (a_core_sems, a_x_sems, a_far_sems),
    )
    sums_b = Sums(
        (b_own, b_core_send, b_core_recv, b_x_send, b_x_recv, b_far_own, b_far_send, b_far_recv),
        (b_core_sems, b_x_sems, b_far_sems),
    )

    def for_sibling(ref, taps):
        for k in range(ROW // 2, ROW):
            at = slice((k - ROW // 2) * group, (k - ROW // 2 + 1) * group)
            for place, tap in enumerate(taps):
                part = dot(summed_pick[tap, k * group : (k + 1) * group, :], gb, NT)
                ref[at, place * width : (place + 1) * width] = part.astype(BF16)

    def for_own(ref, taps):
        for k in range(ROW // 2):
            at = slice(k * group, (k + 1) * group)
            for place, tap in enumerate(taps):
                part = dot(summed_pick[tap, at, :], gb, NT)
                ref[at, place * width : (place + 1) * width] = part

    for_sibling(a_core_send, (0, 1))
    sums_a.to_core()
    gedge_copies = [
        send(gb_ref.at[:, upper], gedge.at[0], gedge_sems, 0, {"seq": right}),
        send(gb_ref.at[:, lower], gedge.at[1], gedge_sems, 1, {"seq": left}),
    ]
    for_sibling(b_core_send, (2,))
    sums_b.to_core()
    top_core_send[...] = dot(hidden_pick[channels // 2 :, :], grad_logits, NN).astype(BF16)
    top_core_copy = send(top_core_send, top_core_recv, top_core_sems, 0, {"seq": core_peer})
    for_own(a_own, (0, 1))
    sums_a.to_x()
    for_own(b_own, (2,))
    sums_b.to_x()
    grad_hidden_ref[...] = grad_hidden
    top_own[...] = dot(hidden_pick[: channels // 2, :], grad_logits, NN)
    wait([top_core_copy])
    for d in range(1, XS):
        at = slice(d * group, (d + 1) * group)
        top_x_send[d - 1] = (top_own[at, :] + top_core_recv[at, :].astype(F32)).astype(BF16)
    top_x_copies = [
        send(top_x_send.at[d - 1], top_x_recv.at[d - 1], top_x_sems, d - 1, {"seq": x_peer[d]})
        for d in range(1, XS)
    ]

    lanes = iota((width, length), 1)
    gb_wide = gb_ref[...].astype(F32)
    to_left = pltpu.roll(gb_wide, length - 1, 1)
    to_right = pltpu.roll(gb_wide, 1, 1)
    shifted[width : 2 * width, :] = gb_ref[...]

    def back_convolution():
        wait(gedge_copies)
        low_edge = gedge[0].astype(F32)[:, half - 1 : half] * keep_low
        high_edge = gedge[1].astype(F32)[:, 0:1] * keep_high
        shifted[0:width, :] = jnp.where(lanes == length - 1, high_edge, to_left).astype(BF16)
        shifted[2 * width :, :] = jnp.where(lanes == 0, low_edge, to_right).astype(BF16)
        copies = []
        for d in (1, 2, 3, 0):
            at = pl.ds(pl.multiple_of(mp_peer[d] * width, width), width)
            total = jnp.zeros((width, length), F32)
            for k in range(3):
                total = total + dot(turned[k, at, :], shifted[k * width : (k + 1) * width, :], NN)
            if d == 0:
                grad_hidden_ref[...] += total
            else:
                back_send[d - 1] = total.astype(BF16)
                copies.append(
                    send(
                        back_send.at[d - 1], back_recv.at[d - 1], back_sems, d - 1,
                        {"mp": mp_peer[d]},
                    )
                )
        return copies

    back_copies = back_convolution()
    sums_a.to_far()
    sums_b.to_far()

    wait(top_x_copies)
    total = top_own[0:group, :] + top_core_recv[0:group, :].astype(F32)
    for d in range(1, XS):
        total = total + top_x_recv[d - 1].astype(F32)
    top_own[0:group, :] = total
    for p in range(1, FAR):
        top_far_send[p - 1, 0:unit, :] = top_own[p * unit : (p + 1) * unit, :].astype(BF16)
    top_far_copies = [
        send(
            top_far_send.at[p - 1], top_far_recv.at[p - 1], top_far_sems, p - 1,
            {"seq": far_peer[p]},
        )
        for p in range(1, FAR)
    ]

    wait(back_copies)
    total = grad_hidden_ref[...]
    for d in range(1, MPS):
        total = total + back_recv[d - 1].astype(F32)
    res_skip[...] = total.astype(BF16)
    stores = [store(res_skip, out_skip, 0)]
    high = total.astype(BF16)
    rest = total - high.astype(F32)
    mid = rest.astype(BF16)
    low = (rest - mid.astype(F32)).astype(BF16)
    pairs = dot(high, spread, NT) + dot(mid, spread, NT) + dot(low, spread, NT)
    res_coarse[...] = pairs.astype(BF16)
    stores.append(store(res_coarse, out_coarse, 1))

    final = sums_a.end()
    for k in range(2):
        res_conv[:, k, :] = final[:, k * width : (k + 1) * width]
    final = sums_b.end()
    res_conv[:, 2, :] = final[:, 0:width]
    stores.append(store(res_conv, out_conv, 3))

    wait(top_far_copies)
    total = top_own[0:16, :]
    for p in range(1, FAR):
        total = total + top_far_recv[p - 1].astype(F32)
    res_head[...] = total[0:unit, :] * scale_back
    stores.append(store(res_head, out_head, 2))
    wait(stores)


def write_out(*refs):
    count = len(refs) // 2
    for k in range(count):
        refs[count + k][...] = refs[k][...]


def shards(coarse, skip, conv_weight, conv_bias, head_weight, head_bias, counts, seg_mask):
    width, length = skip.shape
    channels, tracks = head_weight.shape
    half = length // 2
    group = channels // ROW
    unit = channels // SEQ
    wide = -(-width // 128) * 128

    args = (
        coarse, skip, conv_weight, conv_bias.reshape(1, -1), head_weight,
        head_bias.reshape(1, -1), counts, seg_mask,
    )

    shapes = (
        jax.ShapeDtypeStruct((width, length), BF16),
        jax.ShapeDtypeStruct((width, half), BF16),
        jax.ShapeDtypeStruct((unit, tracks), F32),
        jax.ShapeDtypeStruct((unit, 3, width), F32),
    )

    def sems(count):
        return pltpu.SemaphoreType.DMA((2, count))

    def sums(cols):
        cols = -(-cols // 128) * 128
        packed = -(-unit * (cols // 128) // 16) * 16
        return [
            pltpu.VMEM((channels // 2, cols), F32),
            pltpu.VMEM((channels // 2, cols), BF16),
            pltpu.VMEM((channels // 2, cols), BF16),
            pltpu.VMEM((XS - 1, group, cols), BF16),
            pltpu.VMEM((XS - 1, group, cols), BF16),
            pltpu.VMEM((FAR, packed, 128), F32),
            pltpu.VMEM((FAR - 1, packed, 128), BF16),
            pltpu.VMEM((FAR - 1, packed, 128), BF16),
        ]

    scratch = [pltpu.VMEM(a.shape, a.dtype) for k, a in enumerate(args) if k != 4]
    scratch += [
        pltpu.VMEM((MPS, width, length), BF16),
        pltpu.VMEM((16, wide), BF16),
        pltpu.VMEM((2, MPS, 16, wide), BF16),
        pltpu.VMEM((MPS, 16, wide), BF16),
        pltpu.VMEM((MPS, width, length), BF16),
        pltpu.VMEM((channels, MPS * tracks), BF16),
        pltpu.VMEM((MPS, length, tracks), BF16),
        pltpu.VMEM((ROW, 8, tracks), F32),
        pltpu.VMEM((MPS, 8, tracks), F32),
        pltpu.VMEM((ROW, 8, tracks), F32),
        pltpu.VMEM((width, length), F32),
        pltpu.VMEM((width, length), F32),
        pltpu.VMEM((width, length), BF16),
        pltpu.VMEM((2, width, half), BF16),
        pltpu.VMEM((3 * width, length), BF16),
        pltpu.VMEM((channels, channels), BF16),
        pltpu.VMEM((3, channels, length), BF16),
        pltpu.VMEM((channels, length), BF16),
        pltpu.VMEM((3, channels, width), BF16),
        pltpu.VMEM((MPS - 1, width, length), BF16),
        pltpu.VMEM((MPS - 1, width, length), BF16),
        pltpu.VMEM((channels // 2, tracks), F32),
        pltpu.VMEM((channels // 2, tracks), BF16),
        pltpu.VMEM((channels // 2, tracks), BF16),
        pltpu.VMEM((XS - 1, group, tracks), BF16),
        pltpu.VMEM((XS - 1, group, tracks), BF16),
        pltpu.VMEM((FAR - 1, 16, tracks), BF16),
        pltpu.VMEM((FAR - 1, 16, tracks), BF16),
        *sums(2 * width),
        *sums(width),
        *(pltpu.VMEM(a.shape, a.dtype) for a in shapes),
        pltpu.SemaphoreType.DMA((len(args),)),
        pltpu.SemaphoreType.DMA((len(shapes),)),
        sems(2 * MPS), sems(MPS - 1), sems(2 * MPS - 2), sems(2 * MPS - 2), sems(MPS - 1),
        sems(ROW - 1), sems(MPS - 1), sems(ROW - 1), sems(MPS - 1), sems(ROW - 1),
        sems(2), sems(MPS - 1), sems(1), sems(XS - 1), sems(FAR - 1),
        sems(1), sems(XS - 1), sems(FAR - 1), sems(1), sems(XS - 1), sems(FAR - 1),
    ]
    vmem = pl.BlockSpec(memory_space=pltpu.VMEM)
    hbm = pl.BlockSpec(memory_space=pltpu.HBM)
    results = pl.pallas_call(
        body,
        out_shape=shapes,
        in_specs=[hbm] * len(args),
        out_specs=(hbm,) * len(shapes),
        scratch_shapes=scratch,
        compiler_params=pltpu.CompilerParams(
            collective_id=0, has_side_effects=True, vmem_limit_bytes=VMEM_BYTES
        ),
    )(*args)
    return pl.pallas_call(
        write_out,
        out_shape=shapes,
        in_specs=[vmem] * len(shapes),
        out_specs=(vmem,) * len(shapes),
        compiler_params=pltpu.CompilerParams(vmem_limit_bytes=VMEM_BYTES),
    )(*results)


def solution(mesh):
    in_specs = (
        P("mp", "seq"),
        P("mp", "seq"),
        P(None, "mp", None),
        P("mp"),
        P(None, "mp"),
        P("mp"),
        P("seq", "mp"),
        P(None, "mp"),
    )
    out_specs = (P("mp", "seq"), P("mp", "seq"), P("seq", "mp"), P("seq", None, "mp"))
    return jax.shard_map(shards, mesh=mesh, in_specs=in_specs, out_specs=out_specs, check_vma=False)
```

```python
import functools
import math

import jax
import jax.numpy as jnp
from jax import lax
from jax.experimental import pallas as pl
from jax.experimental.pallas import tpu as pltpu
from jax.sharding import PartitionSpec as P

root_two_pi = 0.7978845608028654
cubic_coef = 0.044715
multi_weight = 5.0
pseudo_count = 0.5

CORES, XS, YS, HIS, MPS = 2, 4, 8, 2, 4
ROW = XS * CORES
FAR = YS * HIS
SEQ = FAR * ROW

F32 = jnp.float32
BF16 = jnp.bfloat16
VMEM_BYTES = 63 * 1024 * 1024
MESH = pl.DeviceIdType.MESH


def gelu_parts(v):
    tangent = jnp.tanh(root_two_pi * (v + cubic_coef * v * v * v))
    value = 0.5 * v * (1.0 + tangent)
    slope = 0.5 * (1.0 + tangent) + 0.5 * v * (1.0 - tangent * tangent) * root_two_pi * (
        1.0 + 3.0 * cubic_coef * v * v
    )
    return value, slope


def dot(left, right, dims):
    return lax.dot_general(left, right, (dims, ((), ())), preferred_element_type=F32)


NN = ((1,), (0,))
NT = ((1,), (1,))
TN = ((0,), (0,))


def iota(shape, axis):
    return lax.broadcasted_iota(jnp.int32, shape, axis)


def one_hot(mask):
    return jnp.where(mask, 1.0, 0.0).astype(BF16)


def body(
    coarse_in, skip_in, weight_in, conv_bias_in, head_in, head_bias_in, counts_in, seg_mask_in,
    out_skip, out_coarse, out_head, out_conv,
    coarse, skip, weight, conv_bias, head_bias, counts, seg_mask,
    summed_all, edge_own, edge_all, mid_all, hidden_all, head_wide, counts_all, count_all,
    small_all, seg_all, slope_ref, grad_hidden_ref, gb_ref, edge_send, edge_recv, shifted,
    pick, summed_pick, hidden_pick, turned,
    back_send, back_recv,
    a_own, a_core_send, a_core_recv, a_x_send, a_x_recv, a_far_own, a_far_send, a_far_recv,
    b_own, b_core_send, b_core_recv, b_x_send, b_x_recv, b_far_own, b_far_send, b_far_recv,
    res_skip, res_coarse, res_head, res_conv,
    in_sems, out_sems, edge_sems, mid_sems, sum_sems, hid_sems, head_sems, spread_sems,
    counts_sems, count_sems, small_sems, seg_sems,
    gedge_sems, back_sems,
    a_core_sems, a_x_sems, a_far_sems, b_core_sems, b_x_sems, b_far_sems,
):
    width, length = skip.shape
    half = length // 2
    channels = head_in.shape[0]
    tracks = head_in.shape[1]
    unit = channels // SEQ
    group = channels // ROW
    scale_back = 1.0 / math.sqrt(length * SEQ)

    s = lax.axis_index("seq")
    z = lax.axis_index("mp")
    core = lax.rem(s, CORES)
    x = lax.rem(s // CORES, XS)
    y = lax.rem(s // ROW, YS)
    hi = s // (ROW * YS)
    mine = lax.rem(s, ROW)

    mp_peer = [lax.rem(z + d, MPS) for d in range(MPS)]
    row_peer = [s - mine + lax.rem(mine + d, ROW) for d in range(ROW)]
    core_peer = s + 1 - 2 * core
    x_peer = [s + CORES * (lax.rem(x + d, XS) - x) for d in range(XS)]
    far_peer = [
        s + ROW * (lax.rem(y + p // HIS, YS) - y) + ROW * YS * (lax.rem(hi + p % HIS, HIS) - hi)
        for p in range(FAR)
    ]
    right = lax.rem(s + 1, SEQ)
    left = lax.rem(s + SEQ - 1, SEQ)

    def send(src, dst, sems, slot, device):
        copy = pltpu.make_async_remote_copy(
            src_ref=src,
            dst_ref=dst,
            send_sem=sems.at[0, slot],
            recv_sem=sems.at[1, slot],
            device_id=device,
            device_id_type=MESH,
        )
        copy.start()
        return copy

    def store(src, dst, slot):
        copy = pltpu.make_async_copy(src, dst, out_sems.at[slot])
        copy.start()
        return copy

    def wait(copies):
        for copy in copies:
            copy.wait()

    barrier = pltpu.get_barrier_semaphore()
    greeted = [{"mp": p} for p in mp_peer[1:]]
    greeted += [{"seq": p, "mp": q} for p in (left, right) for q in mp_peer]
    greeted += [{"seq": p} for p in row_peer[1:] + far_peer[1:]]
    for device in greeted:
        pl.semaphore_signal(barrier, inc=1, device_id=device, device_id_type=MESH)

    loads = []
    for slot, (src, dst) in enumerate(
        (
            (coarse_in, coarse), (skip_in, skip), (head_in, head_wide.at[:, pl.ds(0, tracks)]),
            (counts_in, counts), (weight_in, weight), (conv_bias_in, conv_bias),
            (head_bias_in, head_bias), (seg_mask_in, seg_mask),
        )
    ):
        copy = pltpu.make_async_copy(src, dst, in_sems.at[slot])
        copy.start()
        loads.append(copy)

    spread = one_hot(iota((half, length), 1) // 2 == iota((half, length), 0))
    wait(loads[:2])
    doubled = dot(coarse[...], spread, NN)
    summed = (doubled + skip[...].astype(F32)).astype(BF16)
    summed_all[z] = summed
    shape = (16, length)
    at_row, at_lane = iota(shape, 0), iota(shape, 1)
    ends = [
        one_hot(
            ((at_row == k) & (at_lane == 0))
            | ((at_row == k + 2) & (at_lane == length - 1))
            | ((at_row == k + 4) & (at_lane == half))
        )
        for k in range(2)
    ]
    short = width - 128
    upper_rows = jnp.concatenate([summed[128:, :], jnp.zeros((128 - short, length), BF16)], axis=0)
    edge_own[...] = (dot(ends[0], summed[0:128, :], NT) + dot(ends[1], upper_rows, NT)).astype(BF16)
    mid_all[z] = edge_own[...]
    edge_send[...] = jnp.zeros(edge_send.shape, F32)
    pl.semaphore_wait(barrier, len(greeted))

    lower, upper = pl.ds(0, half), pl.ds(half, half)
    edge_copies = []
    for side, neighbour in ((0, right), (1, left)):
        for d in range(MPS):
            edge_copies.append(
                send(
                    edge_own, edge_all.at[side, z], edge_sems, side * MPS + d,
                    {"seq": neighbour, "mp": mp_peer[d]},
                )
            )
    mid_copies = [
        send(edge_own, mid_all.at[z], mid_sems, d - 1, {"mp": mp_peer[d]}) for d in range(1, MPS)
    ]

    def gather(ref, lanes, sems, first):
        return [
            send(
                ref.at[z, :, lanes], ref.at[z, :, lanes], sems, first + d - 1, {"mp": mp_peer[d]}
            )
            for d in range(1, MPS)
        ]

    sum_low = gather(summed_all, lower, sum_sems, 0)
    wait(loads[2:3])
    my_rows = pl.ds(pl.multiple_of(mine * group, group), group)
    head_copies = [
        send(
            head_wide.at[my_rows, pl.ds(0, tracks)],
            head_wide.at[my_rows, pl.ds((MPS - d) * tracks, tracks)],
            head_sems,
            d - 1,
            {"mp": mp_peer[d]},
        )
        for d in range(1, MPS)
    ]
    sum_high = gather(summed_all, upper, sum_sems, MPS - 1)
    wait(loads[3:])
    observed = counts[...].astype(F32)
    counts_all[0] = observed.astype(BF16)
    count_all[mine] = jnp.zeros(count_all.shape[1:], F32)
    count_all[mine, 0:1, :] = jnp.sum(observed, axis=0, keepdims=True)
    count_copies = [
        send(count_all.at[mine], count_all.at[mine], count_sems, d - 1, {"seq": row_peer[d]})
        for d in range(1, ROW)
    ]

    row = iota((group, channels), 0)
    lane = iota((group, channels), 1)
    step = HIS * unit
    y_step = jnp.zeros_like(row)
    for j in range(1, YS):
        y_step = y_step + jnp.where(row >= step * j, 1, 0)
    rest = row - step * y_step
    hi_step = jnp.where(rest >= unit, 1, 0)
    rest = rest - unit * hi_step
    y_at = y + y_step
    y_at = jnp.where(y_at >= YS, y_at - YS, y_at)
    hi_at = jnp.where(hi_step == 1, 1 - hi, hi)
    base = ((hi_at * YS + y_at) * ROW) * unit + rest
    for c in range(CORES):
        core_at = core if c == 0 else 1 - core
        for d in range(XS):
            x_at = lax.rem(x + d, XS)
            place = (c * XS + d) * group
            pick[place : place + group, :] = one_hot(
                lane == base + (x_at * CORES + core_at) * unit
            )

    for k in range(3):
        turned[k] = weight[k].T
    bias = conv_bias[...]
    part0 = bias.astype(BF16).astype(F32)
    part1 = (bias - part0).astype(BF16).astype(F32)
    part2 = bias - part0 - part1
    at = iota((16, width), 0)
    bias_rows = jnp.where(at == 0, part0, jnp.where(at == 1, part1, jnp.where(at == 2, part2, 0.0)))
    bias_wide = dot(bias_rows.astype(BF16), jnp.ones((16, half), BF16), TN)
    a_far_own[...] = jnp.zeros(a_far_own.shape, F32)
    b_far_own[...] = jnp.zeros(b_far_own.shape, F32)
    b_cols = b_own.shape[1]
    b_own[:, width : b_cols - tracks] = jnp.zeros((channels // 2, b_cols - tracks - width), F32)
    b_core_send[:, width : b_cols - tracks] = jnp.zeros(
        (channels // 2, b_cols - tracks - width), BF16
    )

    wait(edge_copies)
    wait(mid_copies)
    at_row, at_lane = iota((128, channels), 0), iota((128, channels), 1)

    def unpack(ref):
        first = jnp.zeros((16, channels), F32)
        second = jnp.zeros((16, channels), F32)
        for k in range(MPS):
            placed = one_hot(at_lane == at_row + k * width)
            first = first + dot(ref[k], placed, NN)
            placed = one_hot((at_lane == at_row + (k * width + 128)) & (at_row < short))
            second = second + dot(ref[k], placed, NN)
        return first + pltpu.roll(second, 15, 0)

    low_rows = unpack(edge_all.at[0])
    high_rows = unpack(edge_all.at[1])
    mid_rows = unpack(mid_all)
    keep_low = jnp.where(s == 0, 0.0, 1.0)
    keep_high = jnp.where(s == SEQ - 1, 0.0, 1.0)
    low_rows = (low_rows * keep_low).astype(BF16)
    high_rows = (high_rows * keep_high).astype(BF16)
    mid_rows = mid_rows.astype(BF16)
    low_col = dot(weight[0], low_rows, NT)[:, 2:3]
    mid_col = dot(weight[2], mid_rows, NT)[:, 4:5]
    high_col = dot(weight[2], high_rows, NT)[:, 0:1]
    lanes = iota((width, half), 1)

    def convolve(at, first_col, last_col):
        block = summed_all[:, :, at].reshape(channels, half)
        from_low = dot(weight[0], block, NN)
        from_high = dot(weight[2], block, NN)
        before = bias_wide + dot(weight[1], block, NN)
        before = before + jnp.where(lanes == 0, first_col, pltpu.roll(from_low, 1, 1))
        before = before + jnp.where(
            lanes == half - 1, last_col, pltpu.roll(from_high, half - 1, 1)
        )
        value, slope = gelu_parts(before)
        hidden_all[z, :, at] = (summed_all[z, :, at].astype(F32) + value).astype(BF16)
        slope_ref[:, at] = slope
        return from_low[:, half - 1 : half]

    wait(sum_low)
    next_col = convolve(slice(0, half), low_col, mid_col)
    hidden_low = gather(hidden_all, lower, hid_sems, 0)

    wait(head_copies)
    spread_copies = [
        send(
            head_wide.at[my_rows, pl.ds(tracks, (MPS - 1) * tracks)],
            head_wide.at[my_rows, pl.ds(tracks, (MPS - 1) * tracks)],
            spread_sems,
            d - 1,
            {"seq": row_peer[d]},
        )
        for d in range(1, ROW)
    ]

    wait(sum_high)
    convolve(slice(half, length), next_col, high_col)
    hidden_high = gather(hidden_all, upper, hid_sems, MPS - 1)

    wait(count_copies)
    counted = count_all[0]
    for k in range(1, ROW):
        counted = counted + count_all[k]
    small_all[0] = jnp.zeros(small_all.shape[1:], F32)
    small_all[0, 0:1, :] = head_bias[...]
    small_all[0, 1:2, :] = seg_mask[pl.ds(s // ROW, 1), :].astype(F32)
    small_all[0, 2:3, :] = counted[0:1, :]
    small_copies = [
        send(small_all.at[0], small_all.at[MPS - d], small_sems, d - 1, {"mp": mp_peer[d]})
        for d in range(1, MPS)
    ]

    summed_full = summed_all[...].reshape(channels, length)
    lanes_group = iota((group, length), 1)
    for k in range(ROW):
        at = slice(k * group, (k + 1) * group)
        picked = dot(pick[at, :], summed_full, NN)
        low_edge = dot(pick[at, :], low_rows, NT)[:, 2:3]
        high_edge = dot(pick[at, :], high_rows, NT)[:, 0:1]
        summed_pick[0, at, :] = jnp.where(
            lanes_group == 0, low_edge, pltpu.roll(picked, 1, 1)
        ).astype(BF16)
        summed_pick[1, at, :] = picked.astype(BF16)
        summed_pick[2, at, :] = jnp.where(
            lanes_group == length - 1, high_edge, pltpu.roll(picked, length - 1, 1)
        ).astype(BF16)

    for copy in hidden_low + hidden_high:
        copy.wait_send()
    counts_copies = [
        send(counts_all.at[0], counts_all.at[MPS - d], counts_sems, d - 1, {"mp": mp_peer[d]})
        for d in range(1, MPS)
    ]
    wait(small_copies)
    wait(spread_copies)
    for copy in hidden_low + hidden_high:
        copy.wait_recv()
    hidden_full = hidden_all[...].reshape(channels, length)
    products = dot(hidden_full, head_wide[...], TN)
    sigmoids, inverses = [], []
    seg_all[mine] = jnp.zeros(seg_all.shape[1:], F32)
    for d in range(MPS):
        logits = products[:, d * tracks : (d + 1) * tracks] + small_all[d, 0:1, :]
        small = jnp.exp(-jnp.abs(logits))
        predicted = jnp.maximum(logits, 0.0) + jnp.log1p(small) + pseudo_count
        seg_all[mine, d : d + 1, :] = jnp.sum(predicted, axis=0, keepdims=True)
        sigmoids.append((logits, small))
        inverses.append(predicted)
    seg_copies = [
        send(seg_all.at[mine], seg_all.at[mine], seg_sems, d - 1, {"seq": row_peer[d]})
        for d in range(1, ROW)
    ]
    for d in range(MPS):
        logits, small = sigmoids[d]
        sigmoids[d] = small_all[d, 1:2, :] * jnp.where(logits >= 0.0, 1.0, small) / (1.0 + small)
        inverses[d] = multi_weight / inverses[d]
    hidden_pick[...] = dot(pick[...], hidden_full, NN).astype(BF16)
    wait(counts_copies)
    wait(seg_copies)
    totals = seg_all[0]
    for k in range(1, ROW):
        totals = totals + seg_all[k]
    blocks = []
    for d in range(MPS):
        share = 1.0 + (multi_weight - 1.0) * small_all[d, 2:3, :] / totals[d : d + 1, :]
        blocks.append(
            ((share - counts_all[d].astype(F32) * inverses[d]) * sigmoids[d]).astype(BF16)
        )
    grad_logits = blocks[0]
    own_rows = pl.ds(pl.multiple_of(z * width, width), width)
    grad_hidden = dot(head_wide[own_rows, :], jnp.concatenate(blocks, axis=1), NT)
    gb = (grad_hidden * slope_ref[...]).astype(BF16)
    gb_ref[...] = gb

    class Sums:
        def __init__(self, refs, sems):
            self.own, self.core_send, self.core_recv, self.x_send, self.x_recv = refs[:5]
            self.far_own, self.far_send, self.far_recv = refs[5:]
            self.core_sems, self.x_sems, self.far_sems = sems

        def to_core(self):
            self.core_copy = send(
                self.core_send, self.core_recv, self.core_sems, 0, {"seq": core_peer}
            )

        def to_x(self):
            self.core_copy.wait()
            self.x_copies = []
            for d in range(1, XS):
                at = slice(d * group, (d + 1) * group)
                self.x_send[d - 1] = (
                    self.own[at, :] + self.core_recv[at, :].astype(F32)
                ).astype(BF16)
                self.x_copies.append(
                    send(
                        self.x_send.at[d - 1], self.x_recv.at[d - 1], self.x_sems, d - 1,
                        {"seq": x_peer[d]},
                    )
                )
            self.own[0:group, :] += self.core_recv[0:group, :].astype(F32)

        def add_x(self):
            wait(self.x_copies)
            total = self.own[0:group, :]
            for d in range(1, XS):
                total = total + self.x_recv[d - 1].astype(F32)
            self.own[0:group, :] = total

        def to_far(self):
            self.add_x()
            self.far_copies = []
            for p in list(range(1, FAR)) + [0]:
                for j in range(self.own.shape[1] // 128):
                    self.far_own[p, j * unit : (j + 1) * unit, :] = self.own[
                        p * unit : (p + 1) * unit, j * 128 : (j + 1) * 128
                    ]
                if p > 0:
                    self.far_send[p - 1] = self.far_own[p].astype(BF16)
                    self.far_copies.append(
                        send(
                            self.far_send.at[p - 1], self.far_recv.at[p - 1], self.far_sems,
                            p - 1, {"seq": far_peer[p]},
                        )
                    )

        def end(self):
            wait(self.far_copies)
            total = self.far_own[0]
            for p in range(1, FAR):
                total = total + self.far_recv[p - 1].astype(F32)
            total = total * scale_back
            return jnp.concatenate(
                [total[j * unit : (j + 1) * unit, :] for j in range(self.own.shape[1] // 128)],
                axis=1,
            )

    sums_a = Sums(
        (a_own, a_core_send, a_core_recv, a_x_send, a_x_recv, a_far_own, a_far_send, a_far_recv),
        (a_core_sems, a_x_sems, a_far_sems),
    )
    sums_b = Sums(
        (b_own, b_core_send, b_core_recv, b_x_send, b_x_recv, b_far_own, b_far_send, b_far_recv),
        (b_core_sems, b_x_sems, b_far_sems),
    )

    def for_sibling(ref, taps):
        for k in range(ROW // 2, ROW):
            at = slice((k - ROW // 2) * group, (k - ROW // 2 + 1) * group)
            for place, tap in enumerate(taps):
                part = dot(summed_pick[tap, k * group : (k + 1) * group, :], gb, NT)
                ref[at, place * width : (place + 1) * width] = part.astype(BF16)

    def for_own(ref, taps):
        for k in range(ROW // 2):
            at = slice(k * group, (k + 1) * group)
            for place, tap in enumerate(taps):
                part = dot(summed_pick[tap, at, :], gb, NT)
                ref[at, place * width : (place + 1) * width] = part

    for_sibling(a_core_send, (0, 1))
    sums_a.to_core()
    gb_ends = dot(ends[0], gb, NT).astype(BF16)
    for side, tap, at in ((0, 2, 2), (1, 0, 0)):
        term = dot(gb_ends, weight[tap], NN)
        for k in range(MPS):
            edge_send[side, k, 0:1, :] = term[at : at + 1, k * width : k * width + 128]
            edge_send[side, k, 1:2, 0:short] = term[at : at + 1, k * width + 128 : (k + 1) * width]
    gedge_copies = []
    for side, neighbour in ((0, right), (1, left)):
        for d in range(MPS):
            gedge_copies.append(
                send(
                    edge_send.at[side, mp_peer[d]], edge_recv.at[side, z], gedge_sems,
                    side * MPS + d, {"seq": neighbour, "mp": mp_peer[d]},
                )
            )
    for_sibling(b_core_send, (2,))
    b_core_send[:, b_cols - tracks :] = dot(
        hidden_pick[channels // 2 :, :], grad_logits, NN
    ).astype(BF16)
    sums_b.to_core()
    lanes = iota((width, length), 1)
    gb_wide = gb.astype(F32)
    shifted[0:width, :] = jnp.where(
        lanes == length - 1, 0.0, pltpu.roll(gb_wide, length - 1, 1)
    ).astype(BF16)
    shifted[width : 2 * width, :] = gb
    shifted[2 * width :, :] = jnp.where(lanes == 0, 0.0, pltpu.roll(gb_wide, 1, 1)).astype(BF16)

    def back(owner):
        at = pl.ds(pl.multiple_of(owner * width, width), width)
        total = dot(turned[0, at, :], shifted[0:width, :], NN)
        for k in range(1, 3):
            total = total + dot(turned[k, at, :], shifted[k * width : (k + 1) * width, :], NN)
        return total

    back_copies = []
    for d in range(1, MPS):
        back_send[d - 1] = back(mp_peer[d]).astype(BF16)
        back_copies.append(
            send(back_send.at[d - 1], back_recv.at[d - 1], back_sems, d - 1, {"mp": mp_peer[d]})
        )
    for_own(a_own, (0, 1))
    sums_a.to_x()
    for_own(b_own, (2,))
    b_own[:, b_cols - tracks :] = dot(hidden_pick[: channels // 2, :], grad_logits, NN)
    sums_b.to_x()
    grad_hidden_ref[...] = grad_hidden + back(z)
    sums_a.to_far()
    sums_b.to_far()

    wait(back_copies)
    wait(gedge_copies)
    total = grad_hidden_ref[...]
    for side, keep, at in ((0, keep_low, 0), (1, keep_high, length - 1)):
        term = edge_recv[side, 0]
        for k in range(1, MPS):
            term = term + edge_recv[side, k]
        term = (term * keep).T
        term = jnp.concatenate([term[:, 0:1], term[0:short, 1:2]], axis=0)
        total = total + jnp.where(lanes == at, term, 0.0)
    for d in range(1, MPS):
        total = total + back_recv[d - 1].astype(F32)
    res_skip[...] = total.astype(BF16)
    stores = [store(res_skip, out_skip, 0)]
    high = total.astype(BF16)
    rest = total - high.astype(F32)
    mid = rest.astype(BF16)
    low = (rest - mid.astype(F32)).astype(BF16)
    pairs = dot(high, spread, NT) + dot(mid, spread, NT) + dot(low, spread, NT)
    res_coarse[...] = pairs.astype(BF16)
    stores.append(store(res_coarse, out_coarse, 1))

    final = sums_a.end()
    for k in range(2):
        res_conv[:, k, :] = final[:, k * width : (k + 1) * width]
    final = sums_b.end()
    res_conv[:, 2, :] = final[:, 0:width]
    res_head[...] = final[:, b_cols - tracks :]
    stores.append(store(res_head, out_head, 2))
    stores.append(store(res_conv, out_conv, 3))

    wait(stores)


def write_out(*refs):
    count = len(refs) // 2
    for k in range(count):
        refs[count + k][...] = refs[k][...]


def shards(coarse, skip, conv_weight, conv_bias, head_weight, head_bias, counts, seg_mask):
    width, length = skip.shape
    channels, tracks = head_weight.shape
    half = length // 2
    group = channels // ROW
    unit = channels // SEQ

    args = (
        coarse, skip, conv_weight, conv_bias.reshape(1, -1), head_weight,
        head_bias.reshape(1, -1), counts, seg_mask,
    )

    shapes = (
        jax.ShapeDtypeStruct((width, length), BF16),
        jax.ShapeDtypeStruct((width, half), BF16),
        jax.ShapeDtypeStruct((unit, tracks), F32),
        jax.ShapeDtypeStruct((unit, 3, width), F32),
    )

    def sems(count):
        return pltpu.SemaphoreType.DMA((2, count))

    def sums(cols):
        cols = -(-cols // 128) * 128
        packed = -(-unit * (cols // 128) // 16) * 16
        return [
            pltpu.VMEM((channels // 2, cols), F32),
            pltpu.VMEM((channels // 2, cols), BF16),
            pltpu.VMEM((channels // 2, cols), BF16),
            pltpu.VMEM((XS - 1, group, cols), BF16),
            pltpu.VMEM((XS - 1, group, cols), BF16),
            pltpu.VMEM((FAR, packed, 128), F32),
            pltpu.VMEM((FAR - 1, packed, 128), BF16),
            pltpu.VMEM((FAR - 1, packed, 128), BF16),
        ]

    scratch = [pltpu.VMEM(a.shape, a.dtype) for k, a in enumerate(args) if k != 4]
    scratch += [
        pltpu.VMEM((MPS, width, length), BF16),
        pltpu.VMEM((16, 128), BF16),
        pltpu.VMEM((2, MPS, 16, 128), BF16),
        pltpu.VMEM((MPS, 16, 128), BF16),
        pltpu.VMEM((MPS, width, length), BF16),
        pltpu.VMEM((channels, MPS * tracks), BF16),
        pltpu.VMEM((MPS, length, tracks), BF16),
        pltpu.VMEM((ROW, 8, tracks), F32),
        pltpu.VMEM((MPS, 8, tracks), F32),
        pltpu.VMEM((ROW, 8, tracks), F32),
        pltpu.VMEM((width, length), F32),
        pltpu.VMEM((width, length), F32),
        pltpu.VMEM((width, length), BF16),
        pltpu.VMEM((2, MPS, 8, 128), F32),
        pltpu.VMEM((2, MPS, 8, 128), F32),
        pltpu.VMEM((3 * width, length), BF16),
        pltpu.VMEM((channels, channels), BF16),
        pltpu.VMEM((3, channels, length), BF16),
        pltpu.VMEM((channels, length), BF16),
        pltpu.VMEM((3, channels, width), BF16),
        pltpu.VMEM((MPS - 1, width, length), BF16),
        pltpu.VMEM((MPS - 1, width, length), BF16),
        *sums(2 * width),
        *sums(-(-width // 128) * 128 + tracks),
        *(pltpu.VMEM(a.shape, a.dtype) for a in shapes),
        pltpu.SemaphoreType.DMA((len(args),)),
        pltpu.SemaphoreType.DMA((len(shapes),)),
        sems(2 * MPS), sems(MPS - 1), sems(2 * MPS - 2), sems(2 * MPS - 2), sems(MPS - 1),
        sems(ROW - 1), sems(MPS - 1), sems(ROW - 1), sems(MPS - 1), sems(ROW - 1),
        sems(2 * MPS), sems(MPS - 1),
        sems(1), sems(XS - 1), sems(FAR - 1), sems(1), sems(XS - 1), sems(FAR - 1),
    ]
    vmem = pl.BlockSpec(memory_space=pltpu.VMEM)
    hbm = pl.BlockSpec(memory_space=pltpu.HBM)
    results = pl.pallas_call(
        body,
        out_shape=shapes,
        in_specs=[hbm] * len(args),
        out_specs=(hbm,) * len(shapes),
        scratch_shapes=scratch,
        compiler_params=pltpu.CompilerParams(
            collective_id=0, has_side_effects=True, vmem_limit_bytes=VMEM_BYTES
        ),
    )(*args)
    return pl.pallas_call(
        write_out,
        out_shape=shapes,
        in_specs=[vmem] * len(shapes),
        out_specs=(vmem,) * len(shapes),
        compiler_params=pltpu.CompilerParams(vmem_limit_bytes=VMEM_BYTES),
    )(*results)


def solution(mesh):
    in_specs = (
        P("mp", "seq"),
        P("mp", "seq"),
        P(None, "mp", None),
        P("mp"),
        P(None, "mp"),
        P("mp"),
        P("seq", "mp"),
        P(None, "mp"),
    )
    out_specs = (P("mp", "seq"), P("mp", "seq"), P("seq", "mp"), P("seq", None, "mp"))
    return jax.shard_map(shards, mesh=mesh, in_specs=in_specs, out_specs=out_specs, check_vma=False)
```

```python
import functools
import math

import jax
import jax.numpy as jnp
from jax import lax
from jax.experimental import pallas as pl
from jax.experimental.pallas import tpu as pltpu
from jax.sharding import PartitionSpec as P

root_two_pi = 0.7978845608028654
cubic_coef = 0.044715
multi_weight = 5.0
pseudo_count = 0.5

CORES, XS, YS, HIS, MPS = 2, 4, 8, 2, 4
ROW = XS * CORES
FAR = YS * HIS
SEQ = FAR * ROW

F32 = jnp.float32
BF16 = jnp.bfloat16
VMEM_BYTES = 63 * 1024 * 1024
MESH = pl.DeviceIdType.MESH


def gelu_parts(v):
    tangent = jnp.tanh(root_two_pi * (v + cubic_coef * v * v * v))
    value = 0.5 * v * (1.0 + tangent)
    slope = 0.5 * (1.0 + tangent) + 0.5 * v * (1.0 - tangent * tangent) * root_two_pi * (
        1.0 + 3.0 * cubic_coef * v * v
    )
    return value, slope


def dot(left, right, dims):
    return lax.dot_general(left, right, (dims, ((), ())), preferred_element_type=F32)


NN = ((1,), (0,))
NT = ((1,), (1,))
TN = ((0,), (0,))


def iota(shape, axis):
    return lax.broadcasted_iota(jnp.int32, shape, axis)


def one_hot(mask):
    return jnp.where(mask, 1.0, 0.0).astype(BF16)


def body(
    coarse_in, skip_in, weight_in, conv_bias_in, head_in, head_bias_in, counts_in, seg_mask_in,
    out_skip, out_coarse, out_head, out_conv,
    coarse, skip, weight, conv_bias, head_bias, counts, seg_mask,
    summed_all, edge_own, edge_all, mid_all, hidden_all, head_wide, counts_all, count_all,
    small_all, seg_all, slope_ref, grad_hidden_ref, gb_ref, edge_send, edge_recv, shifted,
    pick, summed_pick, hidden_pick, turned,
    back_send, back_recv,
    a_own, a_core_send, a_core_recv, a_x_send, a_x_recv, a_far_own, a_far_send, a_far_recv,
    b_own, b_core_send, b_core_recv, b_x_send, b_x_recv, b_far_own, b_far_send, b_far_recv,
    res_skip, res_coarse, res_head, res_conv,
    in_sems, out_sems, edge_sems, mid_sems, sum_sems, hid_sems, head_sems, spread_sems,
    counts_sems, count_sems, small_sems, seg_sems,
    gedge_sems, back_sems,
    a_core_sems, a_x_sems, a_far_sems, b_core_sems, b_x_sems, b_far_sems,
):
    width, length = skip.shape
    half = length // 2
    channels = head_in.shape[0]
    tracks = head_in.shape[1]
    unit = channels // SEQ
    group = channels // ROW
    scale_back = 1.0 / math.sqrt(length * SEQ)

    s = lax.axis_index("seq")
    z = lax.axis_index("mp")
    core = lax.rem(s, CORES)
    x = lax.rem(s // CORES, XS)
    y = lax.rem(s // ROW, YS)
    hi = s // (ROW * YS)
    mine = lax.rem(s, ROW)

    mp_peer = [lax.rem(z + d, MPS) for d in range(MPS)]
    row_peer = [s - mine + lax.rem(mine + d, ROW) for d in range(ROW)]
    core_peer = s + 1 - 2 * core
    x_peer = [s + CORES * (lax.rem(x + d, XS) - x) for d in range(XS)]
    far_peer = [
        s + ROW * (lax.rem(y + p // HIS, YS) - y) + ROW * YS * (lax.rem(hi + p % HIS, HIS) - hi)
        for p in range(FAR)
    ]
    right = lax.rem(s + 1, SEQ)
    left = lax.rem(s + SEQ - 1, SEQ)

    def send(src, dst, sems, slot, device):
        copy = pltpu.make_async_remote_copy(
            src_ref=src,
            dst_ref=dst,
            send_sem=sems.at[0, slot],
            recv_sem=sems.at[1, slot],
            device_id=device,
            device_id_type=MESH,
        )
        copy.start()
        return copy

    def store(src, dst, slot):
        copy = pltpu.make_async_copy(src, dst, out_sems.at[slot])
        copy.start()
        return copy

    def wait(copies):
        for copy in copies:
            copy.wait()

    barrier = pltpu.get_barrier_semaphore()
    greeted = [{"mp": p} for p in mp_peer[1:]]
    greeted += [{"seq": p, "mp": q} for p in (left, right) for q in mp_peer]
    greeted += [{"seq": p} for p in row_peer[1:] + far_peer[1:]]
    loads = []

    def load(pairs):
        for src, dst in pairs:
            copy = pltpu.make_async_copy(src, dst, in_sems.at[len(loads)])
            copy.start()
            loads.append(copy)

    load(((coarse_in, coarse), (skip_in, skip)))
    for device in greeted:
        pl.semaphore_signal(barrier, inc=1, device_id=device, device_id_type=MESH)
    load(
        (
            (head_in, head_wide.at[:, pl.ds(0, tracks)]), (counts_in, counts),
            (weight_in, weight), (conv_bias_in, conv_bias), (head_bias_in, head_bias),
            (seg_mask_in, seg_mask),
        )
    )

    spread = one_hot(iota((half, length), 1) // 2 == iota((half, length), 0))
    wait(loads[:2])
    doubled = dot(coarse[...], spread, NN)
    summed = (doubled + skip[...].astype(F32)).astype(BF16)
    summed_all[z] = summed
    shape = (16, length)
    at_row, at_lane = iota(shape, 0), iota(shape, 1)
    ends = [
        one_hot(
            ((at_row == k) & (at_lane == 0))
            | ((at_row == k + 2) & (at_lane == length - 1))
            | ((at_row == k + 4) & (at_lane == half))
        )
        for k in range(2)
    ]
    short = width - 128
    upper_rows = jnp.concatenate([summed[128:, :], jnp.zeros((128 - short, length), BF16)], axis=0)
    edge_own[...] = (dot(ends[0], summed[0:128, :], NT) + dot(ends[1], upper_rows, NT)).astype(BF16)
    mid_all[z] = edge_own[...]
    edge_send[...] = jnp.zeros(edge_send.shape, F32)
    pl.semaphore_wait(barrier, len(greeted))

    lower, upper = pl.ds(0, half), pl.ds(half, half)
    edge_copies = []
    for side, neighbour in ((0, right), (1, left)):
        for d in range(MPS):
            edge_copies.append(
                send(
                    edge_own, edge_all.at[side, z], edge_sems, side * MPS + d,
                    {"seq": neighbour, "mp": mp_peer[d]},
                )
            )
    mid_copies = [
        send(edge_own, mid_all.at[z], mid_sems, d - 1, {"mp": mp_peer[d]}) for d in range(1, MPS)
    ]

    def gather(ref, lanes, sems, first):
        return [
            send(
                ref.at[z, :, lanes], ref.at[z, :, lanes], sems, first + d - 1, {"mp": mp_peer[d]}
            )
            for d in range(1, MPS)
        ]

    sum_low = gather(summed_all, lower, sum_sems, 0)
    wait(loads[2:3])
    my_rows = pl.ds(pl.multiple_of(mine * group, group), group)
    head_copies = [
        send(
            head_wide.at[my_rows, pl.ds(0, tracks)],
            head_wide.at[my_rows, pl.ds((MPS - d) * tracks, tracks)],
            head_sems,
            d - 1,
            {"mp": mp_peer[d]},
        )
        for d in range(1, MPS)
    ]
    sum_high = gather(summed_all, upper, sum_sems, MPS - 1)
    wait(loads[3:])
    observed = counts[...].astype(F32)
    counts_all[0] = observed.astype(BF16)
    count_all[mine] = jnp.zeros(count_all.shape[1:], F32)
    count_all[mine, 0:1, :] = jnp.sum(observed, axis=0, keepdims=True)
    count_copies = [
        send(count_all.at[mine], count_all.at[mine], count_sems, d - 1, {"seq": row_peer[d]})
        for d in range(1, ROW)
    ]

    row = iota((group, channels), 0)
    lane = iota((group, channels), 1)
    step = HIS * unit
    y_step = jnp.zeros_like(row)
    for j in range(1, YS):
        y_step = y_step + jnp.where(row >= step * j, 1, 0)
    rest = row - step * y_step
    hi_step = jnp.where(rest >= unit, 1, 0)
    rest = rest - unit * hi_step
    y_at = y + y_step
    y_at = jnp.where(y_at >= YS, y_at - YS, y_at)
    hi_at = jnp.where(hi_step == 1, 1 - hi, hi)
    base = ((hi_at * YS + y_at) * ROW) * unit + rest
    for c in range(CORES):
        core_at = core if c == 0 else 1 - core
        for d in range(XS):
            x_at = lax.rem(x + d, XS)
            place = (c * XS + d) * group
            pick[place : place + group, :] = one_hot(
                lane == base + (x_at * CORES + core_at) * unit
            )

    for k in range(3):
        turned[k] = weight[k].T
    bias = conv_bias[...]
    part0 = bias.astype(BF16).astype(F32)
    part1 = (bias - part0).astype(BF16).astype(F32)
    part2 = bias - part0 - part1
    at = iota((16, width), 0)
    bias_rows = jnp.where(at == 0, part0, jnp.where(at == 1, part1, jnp.where(at == 2, part2, 0.0)))
    bias_wide = dot(bias_rows.astype(BF16), jnp.ones((16, half), BF16), TN)
    a_far_own[...] = jnp.zeros(a_far_own.shape, F32)
    b_far_own[...] = jnp.zeros(b_far_own.shape, F32)
    b_cols = b_own.shape[1]
    b_own[:, width : b_cols - tracks] = jnp.zeros((channels // 2, b_cols - tracks - width), F32)
    b_core_send[:, width : b_cols - tracks] = jnp.zeros(
        (channels // 2, b_cols - tracks - width), BF16
    )

    wait(edge_copies)
    wait(mid_copies)
    def unpack(ref):
        parts = []
        for k in range(MPS):
            tile = ref[k].astype(F32)
            parts += [tile, pltpu.roll(tile, 15, 0)[:, 0:short]]
        return jnp.concatenate(parts, axis=1)

    low_rows = unpack(edge_all.at[0])
    high_rows = unpack(edge_all.at[1])
    mid_rows = unpack(mid_all)
    keep_low = jnp.where(s == 0, 0.0, 1.0)
    keep_high = jnp.where(s == SEQ - 1, 0.0, 1.0)
    low_rows = (low_rows * keep_low).astype(BF16)
    high_rows = (high_rows * keep_high).astype(BF16)
    mid_rows = mid_rows.astype(BF16)
    low_col = dot(weight[0], low_rows, NT)[:, 2:3]
    mid_col = dot(weight[2], mid_rows, NT)[:, 4:5]
    high_col = dot(weight[2], high_rows, NT)[:, 0:1]
    lanes = iota((width, half), 1)

    def convolve(at, first_col, last_col):
        block = summed_all[:, :, at].reshape(channels, half)
        from_low = dot(weight[0], block, NN)
        from_high = dot(weight[2], block, NN)
        before = bias_wide + dot(weight[1], block, NN)
        before = before + jnp.where(lanes == 0, first_col, pltpu.roll(from_low, 1, 1))
        before = before + jnp.where(
            lanes == half - 1, last_col, pltpu.roll(from_high, half - 1, 1)
        )
        value, slope = gelu_parts(before)
        hidden_all[z, :, at] = (summed_all[z, :, at].astype(F32) + value).astype(BF16)
        slope_ref[:, at] = slope
        return from_low[:, half - 1 : half]

    wait(sum_low)
    next_col = convolve(slice(0, half), low_col, mid_col)
    hidden_low = gather(hidden_all, lower, hid_sems, 0)

    wait(head_copies)
    spread_copies = [
        send(
            head_wide.at[my_rows, pl.ds(tracks, (MPS - 1) * tracks)],
            head_wide.at[my_rows, pl.ds(tracks, (MPS - 1) * tracks)],
            spread_sems,
            d - 1,
            {"seq": row_peer[d]},
        )
        for d in range(1, ROW)
    ]

    wait(sum_high)
    convolve(slice(half, length), next_col, high_col)
    hidden_high = gather(hidden_all, upper, hid_sems, MPS - 1)

    wait(count_copies)
    counted = count_all[0]
    for k in range(1, ROW):
        counted = counted + count_all[k]
    small_all[0] = jnp.zeros(small_all.shape[1:], F32)
    small_all[0, 0:1, :] = head_bias[...]
    small_all[0, 1:2, :] = seg_mask[pl.ds(s // ROW, 1), :].astype(F32)
    small_all[0, 2:3, :] = counted[0:1, :]
    small_copies = [
        send(small_all.at[0], small_all.at[MPS - d], small_sems, d - 1, {"mp": mp_peer[d]})
        for d in range(1, MPS)
    ]

    summed_full = summed_all[...].reshape(channels, length)
    lanes_group = iota((group, length), 1)
    for k in range(ROW):
        at = slice(k * group, (k + 1) * group)
        picked = dot(pick[at, :], summed_full, NN)
        low_edge = dot(pick[at, :], low_rows, NT)[:, 2:3]
        high_edge = dot(pick[at, :], high_rows, NT)[:, 0:1]
        summed_pick[0, at, :] = jnp.where(
            lanes_group == 0, low_edge, pltpu.roll(picked, 1, 1)
        ).astype(BF16)
        summed_pick[1, at, :] = picked.astype(BF16)
        summed_pick[2, at, :] = jnp.where(
            lanes_group == length - 1, high_edge, pltpu.roll(picked, length - 1, 1)
        ).astype(BF16)

    wait(small_copies)
    wait(spread_copies)
    wait(hidden_low + hidden_high)
    counts_copies = [
        send(counts_all.at[0], counts_all.at[MPS - d], counts_sems, d - 1, {"mp": mp_peer[d]})
        for d in range(1, MPS)
    ]
    hidden_full = hidden_all[...].reshape(channels, length)
    products = dot(hidden_full, head_wide[...], TN)
    sigmoids, inverses = [], []
    seg_all[mine] = jnp.zeros(seg_all.shape[1:], F32)
    for d in range(MPS):
        logits = products[:, d * tracks : (d + 1) * tracks] + small_all[d, 0:1, :]
        small = jnp.exp(-jnp.abs(logits))
        predicted = jnp.maximum(logits, 0.0) + jnp.log1p(small) + pseudo_count
        seg_all[mine, d : d + 1, :] = jnp.sum(predicted, axis=0, keepdims=True)
        sigmoids.append((logits, small))
        inverses.append(predicted)
    seg_copies = [
        send(seg_all.at[mine], seg_all.at[mine], seg_sems, d - 1, {"seq": row_peer[d]})
        for d in range(1, ROW)
    ]
    for d in range(MPS):
        logits, small = sigmoids[d]
        sigmoids[d] = small_all[d, 1:2, :] * jnp.where(logits >= 0.0, 1.0, small) / (1.0 + small)
        inverses[d] = multi_weight / inverses[d]
    hidden_pick[...] = dot(pick[...], hidden_full, NN).astype(BF16)
    wait(counts_copies)
    wait(seg_copies)
    totals = seg_all[0]
    for k in range(1, ROW):
        totals = totals + seg_all[k]
    blocks = []
    for d in range(MPS):
        share = 1.0 + (multi_weight - 1.0) * small_all[d, 2:3, :] / totals[d : d + 1, :]
        blocks.append(
            ((share - counts_all[d].astype(F32) * inverses[d]) * sigmoids[d]).astype(BF16)
        )
    grad_logits = blocks[0]
    own_rows = pl.ds(pl.multiple_of(z * width, width), width)
    grad_hidden = dot(head_wide[own_rows, :], jnp.concatenate(blocks, axis=1), NT)
    gb = (grad_hidden * slope_ref[...]).astype(BF16)
    gb_ref[...] = gb

    class Sums:
        def __init__(self, refs, sems):
            self.own, self.core_send, self.core_recv, self.x_send, self.x_recv = refs[:5]
            self.far_own, self.far_send, self.far_recv = refs[5:]
            self.core_sems, self.x_sems, self.far_sems = sems

        def to_core(self):
            self.core_copy = send(
                self.core_send, self.core_recv, self.core_sems, 0, {"seq": core_peer}
            )

        def to_x(self):
            self.core_copy.wait()
            self.x_copies = []
            for d in range(1, XS):
                at = slice(d * group, (d + 1) * group)
                self.x_send[d - 1] = (
                    self.own[at, :] + self.core_recv[at, :].astype(F32)
                ).astype(BF16)
                self.x_copies.append(
                    send(
                        self.x_send.at[d - 1], self.x_recv.at[d - 1], self.x_sems, d - 1,
                        {"seq": x_peer[d]},
                    )
                )
            self.own[0:group, :] += self.core_recv[0:group, :].astype(F32)

        def add_x(self):
            wait(self.x_copies)
            total = self.own[0:group, :]
            for d in range(1, XS):
                total = total + self.x_recv[d - 1].astype(F32)
            self.own[0:group, :] = total

        def to_far(self):
            self.add_x()
            self.far_copies = []
            for p in list(range(1, FAR)) + [0]:
                for j in range(self.own.shape[1] // 128):
                    self.far_own[p, j * unit : (j + 1) * unit, :] = self.own[
                        p * unit : (p + 1) * unit, j * 128 : (j + 1) * 128
                    ]
                if p > 0:
                    self.far_send[p - 1] = self.far_own[p].astype(BF16)
                    self.far_copies.append(
                        send(
                            self.far_send.at[p - 1], self.far_recv.at[p - 1], self.far_sems,
                            p - 1, {"seq": far_peer[p]},
                        )
                    )

        def end(self):
            wait(self.far_copies)
            total = self.far_own[0]
            for p in range(1, FAR):
                total = total + self.far_recv[p - 1].astype(F32)
            total = total * scale_back
            return jnp.concatenate(
                [total[j * unit : (j + 1) * unit, :] for j in range(self.own.shape[1] // 128)],
                axis=1,
            )

    sums_a = Sums(
        (a_own, a_core_send, a_core_recv, a_x_send, a_x_recv, a_far_own, a_far_send, a_far_recv),
        (a_core_sems, a_x_sems, a_far_sems),
    )
    sums_b = Sums(
        (b_own, b_core_send, b_core_recv, b_x_send, b_x_recv, b_far_own, b_far_send, b_far_recv),
        (b_core_sems, b_x_sems, b_far_sems),
    )

    def for_sibling(ref, taps):
        for k in range(ROW // 2, ROW):
            at = slice((k - ROW // 2) * group, (k - ROW // 2 + 1) * group)
            for place, tap in enumerate(taps):
                part = dot(summed_pick[tap, k * group : (k + 1) * group, :], gb, NT)
                ref[at, place * width : (place + 1) * width] = part.astype(BF16)

    def for_own(ref, taps):
        for k in range(ROW // 2):
            at = slice(k * group, (k + 1) * group)
            for place, tap in enumerate(taps):
                part = dot(summed_pick[tap, at, :], gb, NT)
                ref[at, place * width : (place + 1) * width] = part

    for_sibling(a_core_send, (0, 1))
    sums_a.to_core()
    gb_ends = dot(ends[0], gb, NT).astype(BF16)
    for side, tap, at in ((0, 2, 2), (1, 0, 0)):
        term = dot(gb_ends, weight[tap], NN)
        for k in range(MPS):
            edge_send[side, k, 0:1, :] = term[at : at + 1, k * width : k * width + 128]
            edge_send[side, k, 1:2, 0:short] = term[at : at + 1, k * width + 128 : (k + 1) * width]
    gedge_copies = []
    for side, neighbour in ((0, right), (1, left)):
        for d in range(MPS):
            gedge_copies.append(
                send(
                    edge_send.at[side, mp_peer[d]], edge_recv.at[side, z], gedge_sems,
                    side * MPS + d, {"seq": neighbour, "mp": mp_peer[d]},
                )
            )
    for_sibling(b_core_send, (2,))
    b_core_send[:, b_cols - tracks :] = dot(
        hidden_pick[channels // 2 :, :], grad_logits, NN
    ).astype(BF16)
    sums_b.to_core()
    lanes = iota((width, length), 1)
    gb_wide = gb.astype(F32)
    shifted[0:width, :] = jnp.where(
        lanes == length - 1, 0.0, pltpu.roll(gb_wide, length - 1, 1)
    ).astype(BF16)
    shifted[width : 2 * width, :] = gb
    shifted[2 * width :, :] = jnp.where(lanes == 0, 0.0, pltpu.roll(gb_wide, 1, 1)).astype(BF16)

    def back(owner):
        at = pl.ds(pl.multiple_of(owner * width, width), width)
        total = dot(turned[0, at, :], shifted[0:width, :], NN)
        for k in range(1, 3):
            total = total + dot(turned[k, at, :], shifted[k * width : (k + 1) * width, :], NN)
        return total

    back_copies = []
    for d in range(1, MPS):
        back_send[d - 1] = back(mp_peer[d]).astype(BF16)
        back_copies.append(
            send(back_send.at[d - 1], back_recv.at[d - 1], back_sems, d - 1, {"mp": mp_peer[d]})
        )
    for_own(a_own, (0, 1))
    sums_a.to_x()
    for_own(b_own, (2,))
    b_own[:, b_cols - tracks :] = dot(hidden_pick[: channels // 2, :], grad_logits, NN)
    sums_b.to_x()
    grad_hidden_ref[...] = grad_hidden + back(z)
    sums_a.to_far()
    sums_b.to_far()

    wait(back_copies)
    wait(gedge_copies)
    total = grad_hidden_ref[...]
    for side, keep, at in ((0, keep_low, 0), (1, keep_high, length - 1)):
        term = edge_recv[side, 0]
        for k in range(1, MPS):
            term = term + edge_recv[side, k]
        term = (term * keep).T
        term = jnp.concatenate([term[:, 0:1], term[0:short, 1:2]], axis=0)
        total = total + jnp.where(lanes == at, term, 0.0)
    for d in range(1, MPS):
        total = total + back_recv[d - 1].astype(F32)
    res_skip[...] = total.astype(BF16)
    stores = [store(res_skip, out_skip, 0)]
    high = total.astype(BF16)
    rest = total - high.astype(F32)
    mid = rest.astype(BF16)
    low = (rest - mid.astype(F32)).astype(BF16)
    pairs = dot(high, spread, NT) + dot(mid, spread, NT) + dot(low, spread, NT)
    res_coarse[...] = pairs.astype(BF16)
    stores.append(store(res_coarse, out_coarse, 1))

    final = sums_a.end()
    for k in range(2):
        res_conv[:, k, :] = final[:, k * width : (k + 1) * width]
    final = sums_b.end()
    res_conv[:, 2, :] = final[:, 0:width]
    res_head[...] = final[:, b_cols - tracks :]
    stores.append(store(res_head, out_head, 2))
    stores.append(store(res_conv, out_conv, 3))

    wait(stores)


def write_out(*refs):
    count = len(refs) // 2
    for k in range(count):
        refs[count + k][...] = refs[k][...]


def shards(coarse, skip, conv_weight, conv_bias, head_weight, head_bias, counts, seg_mask):
    width, length = skip.shape
    channels, tracks = head_weight.shape
    half = length // 2
    group = channels // ROW
    unit = channels // SEQ

    args = (
        coarse, skip, conv_weight, conv_bias.reshape(1, -1), head_weight,
        head_bias.reshape(1, -1), counts, seg_mask,
    )

    shapes = (
        jax.ShapeDtypeStruct((width, length), BF16),
        jax.ShapeDtypeStruct((width, half), BF16),
        jax.ShapeDtypeStruct((unit, tracks), F32),
        jax.ShapeDtypeStruct((unit, 3, width), F32),
    )

    def sems(count):
        return pltpu.SemaphoreType.DMA((2, count))

    def sums(cols):
        cols = -(-cols // 128) * 128
        packed = -(-unit * (cols // 128) // 16) * 16
        return [
            pltpu.VMEM((channels // 2, cols), F32),
            pltpu.VMEM((channels // 2, cols), BF16),
            pltpu.VMEM((channels // 2, cols), BF16),
            pltpu.VMEM((XS - 1, group, cols), BF16),
            pltpu.VMEM((XS - 1, group, cols), BF16),
            pltpu.VMEM((FAR, packed, 128), F32),
            pltpu.VMEM((FAR - 1, packed, 128), BF16),
            pltpu.VMEM((FAR - 1, packed, 128), BF16),
        ]

    scratch = [pltpu.VMEM(a.shape, a.dtype) for k, a in enumerate(args) if k != 4]
    scratch += [
        pltpu.VMEM((MPS, width, length), BF16),
        pltpu.VMEM((16, 128), BF16),
        pltpu.VMEM((2, MPS, 16, 128), BF16),
        pltpu.VMEM((MPS, 16, 128), BF16),
        pltpu.VMEM((MPS, width, length), BF16),
        pltpu.VMEM((channels, MPS * tracks), BF16),
        pltpu.VMEM((MPS, length, tracks), BF16),
        pltpu.VMEM((ROW, 8, tracks), F32),
        pltpu.VMEM((MPS, 8, tracks), F32),
        pltpu.VMEM((ROW, 8, tracks), F32),
        pltpu.VMEM((width, length), F32),
        pltpu.VMEM((width, length), F32),
        pltpu.VMEM((width, length), BF16),
        pltpu.VMEM((2, MPS, 8, 128), F32),
        pltpu.VMEM((2, MPS, 8, 128), F32),
        pltpu.VMEM((3 * width, length), BF16),
        pltpu.VMEM((channels, channels), BF16),
        pltpu.VMEM((3, channels, length), BF16),
        pltpu.VMEM((channels, length), BF16),
        pltpu.VMEM((3, channels, width), BF16),
        pltpu.VMEM((MPS - 1, width, length), BF16),
        pltpu.VMEM((MPS - 1, width, length), BF16),
        *sums(2 * width),
        *sums(-(-width // 128) * 128 + tracks),
        *(pltpu.VMEM(a.shape, a.dtype) for a in shapes),
        pltpu.SemaphoreType.DMA((len(args),)),
        pltpu.SemaphoreType.DMA((len(shapes),)),
        sems(2 * MPS), sems(MPS - 1), sems(2 * MPS - 2), sems(2 * MPS - 2), sems(MPS - 1),
        sems(ROW - 1), sems(MPS - 1), sems(ROW - 1), sems(MPS - 1), sems(ROW - 1),
        sems(2 * MPS), sems(MPS - 1),
        sems(1), sems(XS - 1), sems(FAR - 1), sems(1), sems(XS - 1), sems(FAR - 1),
    ]
    vmem = pl.BlockSpec(memory_space=pltpu.VMEM)
    hbm = pl.BlockSpec(memory_space=pltpu.HBM)
    results = pl.pallas_call(
        body,
        out_shape=shapes,
        in_specs=[hbm] * len(args),
        out_specs=(hbm,) * len(shapes),
        scratch_shapes=scratch,
        compiler_params=pltpu.CompilerParams(
            collective_id=0, has_side_effects=True, vmem_limit_bytes=VMEM_BYTES
        ),
    )(*args)
    return pl.pallas_call(
        write_out,
        out_shape=shapes,
        in_specs=[vmem] * len(shapes),
        out_specs=(vmem,) * len(shapes),
        compiler_params=pltpu.CompilerParams(vmem_limit_bytes=VMEM_BYTES),
    )(*results)


def solution(mesh):
    in_specs = (
        P("mp", "seq"),
        P("mp", "seq"),
        P(None, "mp", None),
        P("mp"),
        P(None, "mp"),
        P("mp"),
        P("seq", "mp"),
        P(None, "mp"),
    )
    out_specs = (P("mp", "seq"), P("mp", "seq"), P("seq", "mp"), P("seq", None, "mp"))
    return jax.shard_map(shards, mesh=mesh, in_specs=in_specs, out_specs=out_specs, check_vma=False)
```

```python
import functools
import math

import jax
import jax.numpy as jnp
from jax import lax
from jax.experimental import pallas as pl
from jax.experimental.pallas import tpu as pltpu
from jax.sharding import PartitionSpec as P

root_two_pi = 0.7978845608028654
cubic_coef = 0.044715
multi_weight = 5.0
pseudo_count = 0.5

CORES, XS, YS, HIS, MPS = 2, 4, 8, 2, 4
ROW = XS * CORES
FAR = YS * HIS
SEQ = FAR * ROW

F32 = jnp.float32
BF16 = jnp.bfloat16
VMEM_BYTES = 63 * 1024 * 1024
MESH = pl.DeviceIdType.MESH


def gelu_parts(v):
    tangent = jnp.tanh(root_two_pi * (v + cubic_coef * v * v * v))
    value = 0.5 * v * (1.0 + tangent)
    slope = 0.5 * (1.0 + tangent) + 0.5 * v * (1.0 - tangent * tangent) * root_two_pi * (
        1.0 + 3.0 * cubic_coef * v * v
    )
    return value, slope


def dot(left, right, dims):
    return lax.dot_general(left, right, (dims, ((), ())), preferred_element_type=F32)


NN = ((1,), (0,))
NT = ((1,), (1,))
TN = ((0,), (0,))


def iota(shape, axis):
    return lax.broadcasted_iota(jnp.int32, shape, axis)


def one_hot(mask):
    return jnp.where(mask, 1.0, 0.0).astype(BF16)


def body(
    coarse_in, skip_in, weight_in, conv_bias_in, head_in, head_bias_in, counts_in, seg_mask_in,
    out_skip, out_coarse, out_head, out_conv,
    coarse, skip, weight, conv_bias, head_bias, counts, seg_mask,
    summed_all, edge_own, edge_all, mid_all, hidden_all, head_wide, counts_all, count_all,
    small_all, seg_all, slope_ref, grad_hidden_ref, gb_ref, edge_send, edge_recv, shifted,
    pick, summed_pick, hidden_pick, turned,
    back_send, back_recv,
    a_own, a_core_send, a_core_recv, a_x_send, a_x_recv, a_far_own, a_far_send, a_far_recv,
    b_own, b_core_send, b_core_recv, b_x_send, b_x_recv, b_far_own, b_far_send, b_far_recv,
    res_skip, res_coarse, res_head, res_conv,
    in_sems, out_sems, edge_sems, mid_sems, sum_sems, hid_sems, head_sems, spread_sems,
    counts_sems, count_sems, small_sems, seg_sems,
    gedge_sems, back_sems,
    a_core_sems, a_x_sems, a_far_sems, b_core_sems, b_x_sems, b_far_sems,
):
    width, length = skip.shape
    half = length // 2
    channels = head_in.shape[0]
    tracks = head_in.shape[1]
    unit = channels // SEQ
    group = channels // ROW
    scale_back = 1.0 / math.sqrt(length * SEQ)

    s = lax.axis_index("seq")
    z = lax.axis_index("mp")
    core = lax.rem(s, CORES)
    x = lax.rem(s // CORES, XS)
    y = lax.rem(s // ROW, YS)
    hi = s // (ROW * YS)
    mine = lax.rem(s, ROW)

    mp_peer = [lax.rem(z + d, MPS) for d in range(MPS)]
    row_peer = [s - mine + lax.rem(mine + d, ROW) for d in range(ROW)]
    core_peer = s + 1 - 2 * core
    x_peer = [s + CORES * (lax.rem(x + d, XS) - x) for d in range(XS)]
    far_peer = [
        s + ROW * (lax.rem(y + p // HIS, YS) - y) + ROW * YS * (lax.rem(hi + p % HIS, HIS) - hi)
        for p in range(FAR)
    ]
    right = lax.rem(s + 1, SEQ)
    left = lax.rem(s + SEQ - 1, SEQ)

    def send(src, dst, sems, slot, device):
        copy = pltpu.make_async_remote_copy(
            src_ref=src,
            dst_ref=dst,
            send_sem=sems.at[0, slot],
            recv_sem=sems.at[1, slot],
            device_id=device,
            device_id_type=MESH,
        )
        copy.start()
        return copy

    def store(src, dst, slot):
        copy = pltpu.make_async_copy(src, dst, out_sems.at[slot])
        copy.start()
        return copy

    def wait(copies):
        for copy in copies:
            copy.wait()

    barrier = pltpu.get_barrier_semaphore()
    greeted = [{"mp": p} for p in mp_peer[1:]]
    greeted += [{"seq": p, "mp": q} for p in (left, right) for q in mp_peer]
    greeted += [{"seq": p} for p in row_peer[1:] + far_peer[1:]]
    loads = []

    def load(pairs):
        for src, dst in pairs:
            copy = pltpu.make_async_copy(src, dst, in_sems.at[len(loads)])
            copy.start()
            loads.append(copy)

    load(((coarse_in, coarse), (skip_in, skip)))
    for device in greeted:
        pl.semaphore_signal(barrier, inc=1, device_id=device, device_id_type=MESH)
    load(
        (
            (head_in, head_wide.at[:, pl.ds(0, tracks)]), (counts_in, counts),
            (weight_in, weight), (conv_bias_in, conv_bias), (head_bias_in, head_bias),
            (seg_mask_in, seg_mask),
        )
    )

    spread = one_hot(iota((half, length), 1) // 2 == iota((half, length), 0))
    wait(loads[:2])
    doubled = dot(coarse[...], spread, NN)
    summed = (doubled + skip[...].astype(F32)).astype(BF16)
    summed_all[z] = summed
    shape = (16, length)
    at_row, at_lane = iota(shape, 0), iota(shape, 1)
    ends = [
        one_hot(
            ((at_row == k) & (at_lane == 0))
            | ((at_row == k + 2) & (at_lane == length - 1))
            | ((at_row == k + 4) & (at_lane == half))
        )
        for k in range(2)
    ]
    short = width - 128
    upper_rows = jnp.concatenate([summed[128:, :], jnp.zeros((128 - short, length), BF16)], axis=0)
    edge_own[...] = (dot(ends[0], summed[0:128, :], NT) + dot(ends[1], upper_rows, NT)).astype(BF16)
    mid_all[z] = edge_own[...]
    edge_send[...] = jnp.zeros(edge_send.shape, F32)
    pl.semaphore_wait(barrier, len(greeted))

    lower, upper = pl.ds(0, half), pl.ds(half, half)
    edge_copies = []
    for side, neighbour in ((0, right), (1, left)):
        for d in range(MPS):
            edge_copies.append(
                send(
                    edge_own, edge_all.at[side, z], edge_sems, side * MPS + d,
                    {"seq": neighbour, "mp": mp_peer[d]},
                )
            )
    mid_copies = [
        send(edge_own, mid_all.at[z], mid_sems, d - 1, {"mp": mp_peer[d]}) for d in range(1, MPS)
    ]

    def gather(ref, lanes, sems, first):
        return [
            send(
                ref.at[z, :, lanes], ref.at[z, :, lanes], sems, first + d - 1, {"mp": mp_peer[d]}
            )
            for d in range(1, MPS)
        ]

    sum_low = gather(summed_all, lower, sum_sems, 0)
    wait(loads[2:3])
    my_rows = pl.ds(pl.multiple_of(mine * group, group), group)
    head_copies = [
        send(
            head_wide.at[my_rows, pl.ds(0, tracks)],
            head_wide.at[my_rows, pl.ds((MPS - d) * tracks, tracks)],
            head_sems,
            d - 1,
            {"mp": mp_peer[d]},
        )
        for d in range(1, MPS)
    ]
    sum_high = gather(summed_all, upper, sum_sems, MPS - 1)
    wait(loads[3:])
    observed = counts[...].astype(F32)
    counts_all[0] = observed.astype(BF16)
    count_all[mine] = jnp.zeros(count_all.shape[1:], F32)
    count_all[mine, 0:1, :] = jnp.sum(observed, axis=0, keepdims=True)
    count_copies = [
        send(count_all.at[mine], count_all.at[mine], count_sems, d - 1, {"seq": row_peer[d]})
        for d in range(1, ROW)
    ]

    row = iota((group, channels), 0)
    lane = iota((group, channels), 1)
    step = HIS * unit
    y_step = jnp.zeros_like(row)
    for j in range(1, YS):
        y_step = y_step + jnp.where(row >= step * j, 1, 0)
    rest = row - step * y_step
    hi_step = jnp.where(rest >= unit, 1, 0)
    rest = rest - unit * hi_step
    y_at = y + y_step
    y_at = jnp.where(y_at >= YS, y_at - YS, y_at)
    hi_at = jnp.where(hi_step == 1, 1 - hi, hi)
    base = ((hi_at * YS + y_at) * ROW) * unit + rest
    for c in range(CORES):
        core_at = core if c == 0 else 1 - core
        for d in range(XS):
            x_at = lax.rem(x + d, XS)
            place = (c * XS + d) * group
            pick[place : place + group, :] = one_hot(
                lane == base + (x_at * CORES + core_at) * unit
            )

    for k in range(3):
        turned[k] = weight[k].T
    bias = conv_bias[...]
    part0 = bias.astype(BF16).astype(F32)
    part1 = (bias - part0).astype(BF16).astype(F32)
    part2 = bias - part0 - part1
    at = iota((16, width), 0)
    bias_rows = jnp.where(at == 0, part0, jnp.where(at == 1, part1, jnp.where(at == 2, part2, 0.0)))
    bias_wide = dot(bias_rows.astype(BF16), jnp.ones((16, half), BF16), TN)
    a_far_own[...] = jnp.zeros(a_far_own.shape, F32)
    b_far_own[...] = jnp.zeros(b_far_own.shape, F32)
    b_cols = b_own.shape[1]
    b_own[:, width : b_cols - tracks] = jnp.zeros((channels // 2, b_cols - tracks - width), F32)
    b_core_send[:, width : b_cols - tracks] = jnp.zeros(
        (channels // 2, b_cols - tracks - width), BF16
    )

    wait(edge_copies)
    wait(mid_copies)
    def unpack(ref):
        parts = []
        for k in range(MPS):
            tile = ref[k].astype(F32)
            parts += [tile, pltpu.roll(tile, 15, 0)[:, 0:short]]
        return jnp.concatenate(parts, axis=1)

    low_rows = unpack(edge_all.at[0])
    high_rows = unpack(edge_all.at[1])
    mid_rows = unpack(mid_all)
    keep_low = jnp.where(s == 0, 0.0, 1.0)
    keep_high = jnp.where(s == SEQ - 1, 0.0, 1.0)
    low_rows = (low_rows * keep_low).astype(BF16)
    high_rows = (high_rows * keep_high).astype(BF16)
    mid_rows = mid_rows.astype(BF16)
    low_col = dot(weight[0], low_rows, NT)[:, 2:3]
    mid_col = dot(weight[2], mid_rows, NT)[:, 4:5]
    high_col = dot(weight[2], high_rows, NT)[:, 0:1]
    lanes = iota((width, half), 1)

    def convolve(at, first_col, last_col):
        block = summed_all[:, :, at].reshape(channels, half)
        from_low = dot(weight[0], block, NN)
        from_high = dot(weight[2], block, NN)
        before = bias_wide + dot(weight[1], block, NN)
        before = before + jnp.where(lanes == 0, first_col, pltpu.roll(from_low, 1, 1))
        before = before + jnp.where(
            lanes == half - 1, last_col, pltpu.roll(from_high, half - 1, 1)
        )
        value, slope = gelu_parts(before)
        hidden_all[z, :, at] = (summed_all[z, :, at].astype(F32) + value).astype(BF16)
        slope_ref[:, at] = slope
        return from_low[:, half - 1 : half]

    wait(sum_low)
    next_col = convolve(slice(0, half), low_col, mid_col)
    hidden_low = gather(hidden_all, lower, hid_sems, 0)

    wait(head_copies)
    spread_copies = [
        send(
            head_wide.at[my_rows, pl.ds(tracks, (MPS - 1) * tracks)],
            head_wide.at[my_rows, pl.ds(tracks, (MPS - 1) * tracks)],
            spread_sems,
            d - 1,
            {"seq": row_peer[d]},
        )
        for d in range(1, ROW)
    ]

    wait(sum_high)
    convolve(slice(half, length), next_col, high_col)
    hidden_high = gather(hidden_all, upper, hid_sems, MPS - 1)

    wait(count_copies)
    counted = count_all[0]
    for k in range(1, ROW):
        counted = counted + count_all[k]
    small_all[0] = jnp.zeros(small_all.shape[1:], F32)
    small_all[0, 0:1, :] = head_bias[...]
    small_all[0, 1:2, :] = seg_mask[pl.ds(s // ROW, 1), :].astype(F32)
    small_all[0, 2:3, :] = counted[0:1, :]
    small_copies = [
        send(small_all.at[0], small_all.at[MPS - d], small_sems, d - 1, {"mp": mp_peer[d]})
        for d in range(1, MPS)
    ]

    summed_full = summed_all[...].reshape(channels, length)
    lanes_group = iota((group, length), 1)
    for k in range(ROW):
        at = slice(k * group, (k + 1) * group)
        picked = dot(pick[at, :], summed_full, NN)
        low_edge = dot(pick[at, :], low_rows, NT)[:, 2:3]
        high_edge = dot(pick[at, :], high_rows, NT)[:, 0:1]
        summed_pick[0, at, :] = jnp.where(
            lanes_group == 0, low_edge, pltpu.roll(picked, 1, 1)
        ).astype(BF16)
        summed_pick[1, at, :] = picked.astype(BF16)
        summed_pick[2, at, :] = jnp.where(
            lanes_group == length - 1, high_edge, pltpu.roll(picked, length - 1, 1)
        ).astype(BF16)

    wait(small_copies)
    wait(spread_copies)
    wait(hidden_low + hidden_high)
    counts_copies = [
        send(counts_all.at[0], counts_all.at[MPS - d], counts_sems, d - 1, {"mp": mp_peer[d]})
        for d in range(1, MPS)
    ]
    hidden_full = hidden_all[...].reshape(channels, length)
    products = dot(hidden_full, head_wide[...], TN)
    sigmoids, inverses = [], []
    seg_all[mine] = jnp.zeros(seg_all.shape[1:], F32)
    for d in range(MPS):
        logits = products[:, d * tracks : (d + 1) * tracks] + small_all[d, 0:1, :]
        small = jnp.exp(-jnp.abs(logits))
        predicted = jnp.maximum(logits, 0.0) + jnp.log1p(small) + pseudo_count
        seg_all[mine, d : d + 1, :] = jnp.sum(predicted, axis=0, keepdims=True)
        sigmoids.append((logits, small))
        inverses.append(predicted)
    seg_copies = [
        send(seg_all.at[mine], seg_all.at[mine], seg_sems, d - 1, {"seq": row_peer[d]})
        for d in range(1, ROW)
    ]
    for d in range(MPS):
        logits, small = sigmoids[d]
        sigmoids[d] = small_all[d, 1:2, :] * jnp.where(logits >= 0.0, 1.0, small) / (1.0 + small)
        inverses[d] = multi_weight / inverses[d]
    hidden_pick[...] = dot(pick[...], hidden_full, NN).astype(BF16)
    wait(counts_copies)
    wait(seg_copies)
    totals = seg_all[0]
    for k in range(1, ROW):
        totals = totals + seg_all[k]
    blocks = []
    for d in range(MPS):
        share = 1.0 + (multi_weight - 1.0) * small_all[d, 2:3, :] / totals[d : d + 1, :]
        blocks.append(
            ((share - counts_all[d].astype(F32) * inverses[d]) * sigmoids[d]).astype(BF16)
        )
    grad_logits = blocks[0]
    own_rows = pl.ds(pl.multiple_of(z * width, width), width)
    grad_hidden = dot(head_wide[own_rows, :], jnp.concatenate(blocks, axis=1), NT)
    gb = (grad_hidden * slope_ref[...]).astype(BF16)
    gb_ref[...] = gb

    class Sums:
        def __init__(self, refs, sems):
            self.own, self.core_send, self.core_recv, self.x_send, self.x_recv = refs[:5]
            self.far_own, self.far_send, self.far_recv = refs[5:]
            self.core_sems, self.x_sems, self.far_sems = sems

        def to_core(self):
            self.core_copy = send(
                self.core_send, self.core_recv, self.core_sems, 0, {"seq": core_peer}
            )

        def to_x(self):
            self.core_copy.wait()
            self.x_copies = []
            for d in range(1, XS):
                at = slice(d * group, (d + 1) * group)
                self.x_send[d - 1] = (
                    self.own[at, :] + self.core_recv[at, :].astype(F32)
                ).astype(BF16)
                self.x_copies.append(
                    send(
                        self.x_send.at[d - 1], self.x_recv.at[d - 1], self.x_sems, d - 1,
                        {"seq": x_peer[d]},
                    )
                )
            self.own[0:group, :] += self.core_recv[0:group, :].astype(F32)

        def add_x(self):
            wait(self.x_copies)
            total = self.own[0:group, :]
            for d in range(1, XS):
                total = total + self.x_recv[d - 1].astype(F32)
            self.own[0:group, :] = total

        def to_far(self):
            self.add_x()
            self.far_copies = []
            for p in list(range(1, FAR)) + [0]:
                for j in range(self.own.shape[1] // 128):
                    self.far_own[p, j * unit : (j + 1) * unit, :] = self.own[
                        p * unit : (p + 1) * unit, j * 128 : (j + 1) * 128
                    ]
                if p > 0:
                    self.far_send[p - 1] = self.far_own[p].astype(BF16)
                    self.far_copies.append(
                        send(
                            self.far_send.at[p - 1], self.far_recv.at[p - 1], self.far_sems,
                            p - 1, {"seq": far_peer[p]},
                        )
                    )

        def end(self):
            wait(self.far_copies)
            total = self.far_own[0]
            for p in range(1, FAR):
                total = total + self.far_recv[p - 1].astype(F32)
            total = total * scale_back
            return jnp.concatenate(
                [total[j * unit : (j + 1) * unit, :] for j in range(self.own.shape[1] // 128)],
                axis=1,
            )

    sums_a = Sums(
        (a_own, a_core_send, a_core_recv, a_x_send, a_x_recv, a_far_own, a_far_send, a_far_recv),
        (a_core_sems, a_x_sems, a_far_sems),
    )
    sums_b = Sums(
        (b_own, b_core_send, b_core_recv, b_x_send, b_x_recv, b_far_own, b_far_send, b_far_recv),
        (b_core_sems, b_x_sems, b_far_sems),
    )

    def for_sibling(ref, taps):
        for k in range(ROW // 2, ROW):
            at = slice((k - ROW // 2) * group, (k - ROW // 2 + 1) * group)
            for place, tap in enumerate(taps):
                part = dot(summed_pick[tap, k * group : (k + 1) * group, :], gb, NT)
                ref[at, place * width : (place + 1) * width] = part.astype(BF16)

    def for_own(ref, taps):
        for k in range(ROW // 2):
            at = slice(k * group, (k + 1) * group)
            for place, tap in enumerate(taps):
                part = dot(summed_pick[tap, at, :], gb, NT)
                ref[at, place * width : (place + 1) * width] = part

    for_sibling(a_core_send, (0, 1))
    sums_a.to_core()
    for_sibling(b_core_send, (2,))
    b_core_send[:, b_cols - tracks :] = dot(
        hidden_pick[channels // 2 :, :], grad_logits, NN
    ).astype(BF16)
    sums_b.to_core()
    for_own(a_own, (0, 1))
    sums_a.to_x()
    for_own(b_own, (2,))
    b_own[:, b_cols - tracks :] = dot(hidden_pick[: channels // 2, :], grad_logits, NN)
    sums_b.to_x()
    gb_ends = dot(ends[0], gb, NT).astype(BF16)
    for side, tap, at in ((0, 2, 2), (1, 0, 0)):
        term = dot(gb_ends, weight[tap], NN)
        for k in range(MPS):
            edge_send[side, k, 0:1, :] = term[at : at + 1, k * width : k * width + 128]
            edge_send[side, k, 1:2, 0:short] = term[at : at + 1, k * width + 128 : (k + 1) * width]
    gedge_copies = []
    for side, neighbour in ((0, right), (1, left)):
        for d in range(MPS):
            gedge_copies.append(
                send(
                    edge_send.at[side, mp_peer[d]], edge_recv.at[side, z], gedge_sems,
                    side * MPS + d, {"seq": neighbour, "mp": mp_peer[d]},
                )
            )
    lanes = iota((width, length), 1)
    gb_wide = gb.astype(F32)
    shifted[0:width, :] = jnp.where(
        lanes == length - 1, 0.0, pltpu.roll(gb_wide, length - 1, 1)
    ).astype(BF16)
    shifted[width : 2 * width, :] = gb
    shifted[2 * width :, :] = jnp.where(lanes == 0, 0.0, pltpu.roll(gb_wide, 1, 1)).astype(BF16)

    def back(owner):
        at = pl.ds(pl.multiple_of(owner * width, width), width)
        total = dot(turned[0, at, :], shifted[0:width, :], NN)
        for k in range(1, 3):
            total = total + dot(turned[k, at, :], shifted[k * width : (k + 1) * width, :], NN)
        return total

    back_copies = []
    for d in range(1, MPS):
        back_send[d - 1] = back(mp_peer[d]).astype(BF16)
        back_copies.append(
            send(back_send.at[d - 1], back_recv.at[d - 1], back_sems, d - 1, {"mp": mp_peer[d]})
        )
    grad_hidden_ref[...] = grad_hidden + back(z)
    sums_a.to_far()
    sums_b.to_far()

    wait(back_copies)
    wait(gedge_copies)
    total = grad_hidden_ref[...]
    for side, keep, at in ((0, keep_low, 0), (1, keep_high, length - 1)):
        term = edge_recv[side, 0]
        for k in range(1, MPS):
            term = term + edge_recv[side, k]
        term = (term * keep).T
        term = jnp.concatenate([term[:, 0:1], term[0:short, 1:2]], axis=0)
        total = total + jnp.where(lanes == at, term, 0.0)
    for d in range(1, MPS):
        total = total + back_recv[d - 1].astype(F32)
    res_skip[...] = total.astype(BF16)
    stores = [store(res_skip, out_skip, 0)]
    high = total.astype(BF16)
    rest = total - high.astype(F32)
    mid = rest.astype(BF16)
    low = (rest - mid.astype(F32)).astype(BF16)
    pairs = dot(high, spread, NT) + dot(mid, spread, NT) + dot(low, spread, NT)
    res_coarse[...] = pairs.astype(BF16)
    stores.append(store(res_coarse, out_coarse, 1))

    final = sums_a.end()
    for k in range(2):
        res_conv[:, k, :] = final[:, k * width : (k + 1) * width]
    final = sums_b.end()
    res_conv[:, 2, :] = final[:, 0:width]
    res_head[...] = final[:, b_cols - tracks :]
    stores.append(store(res_head, out_head, 2))
    stores.append(store(res_conv, out_conv, 3))

    wait(stores)


def write_out(*refs):
    count = len(refs) // 2
    for k in range(count):
        refs[count + k][...] = refs[k][...]


def shards(coarse, skip, conv_weight, conv_bias, head_weight, head_bias, counts, seg_mask):
    width, length = skip.shape
    channels, tracks = head_weight.shape
    half = length // 2
    group = channels // ROW
    unit = channels // SEQ

    args = (
        coarse, skip, conv_weight, conv_bias.reshape(1, -1), head_weight,
        head_bias.reshape(1, -1), counts, seg_mask,
    )

    shapes = (
        jax.ShapeDtypeStruct((width, length), BF16),
        jax.ShapeDtypeStruct((width, half), BF16),
        jax.ShapeDtypeStruct((unit, tracks), F32),
        jax.ShapeDtypeStruct((unit, 3, width), F32),
    )

    def sems(count):
        return pltpu.SemaphoreType.DMA((2, count))

    def sums(cols):
        cols = -(-cols // 128) * 128
        packed = -(-unit * (cols // 128) // 16) * 16
        return [
            pltpu.VMEM((channels // 2, cols), F32),
            pltpu.VMEM((channels // 2, cols), BF16),
            pltpu.VMEM((channels // 2, cols), BF16),
            pltpu.VMEM((XS - 1, group, cols), BF16),
            pltpu.VMEM((XS - 1, group, cols), BF16),
            pltpu.VMEM((FAR, packed, 128), F32),
            pltpu.VMEM((FAR - 1, packed, 128), BF16),
            pltpu.VMEM((FAR - 1, packed, 128), BF16),
        ]

    scratch = [pltpu.VMEM(a.shape, a.dtype) for k, a in enumerate(args) if k != 4]
    scratch += [
        pltpu.VMEM((MPS, width, length), BF16),
        pltpu.VMEM((16, 128), BF16),
        pltpu.VMEM((2, MPS, 16, 128), BF16),
        pltpu.VMEM((MPS, 16, 128), BF16),
        pltpu.VMEM((MPS, width, length), BF16),
        pltpu.VMEM((channels, MPS * tracks), BF16),
        pltpu.VMEM((MPS, length, tracks), BF16),
        pltpu.VMEM((ROW, 8, tracks), F32),
        pltpu.VMEM((MPS, 8, tracks), F32),
        pltpu.VMEM((ROW, 8, tracks), F32),
        pltpu.VMEM((width, length), F32),
        pltpu.VMEM((width, length), F32),
        pltpu.VMEM((width, length), BF16),
        pltpu.VMEM((2, MPS, 8, 128), F32),
        pltpu.VMEM((2, MPS, 8, 128), F32),
        pltpu.VMEM((3 * width, length), BF16),
        pltpu.VMEM((channels, channels), BF16),
        pltpu.VMEM((3, channels, length), BF16),
        pltpu.VMEM((channels, length), BF16),
        pltpu.VMEM((3, channels, width), BF16),
        pltpu.VMEM((MPS - 1, width, length), BF16),
        pltpu.VMEM((MPS - 1, width, length), BF16),
        *sums(2 * width),
        *sums(-(-width // 128) * 128 + tracks),
        *(pltpu.VMEM(a.shape, a.dtype) for a in shapes),
        pltpu.SemaphoreType.DMA((len(args),)),
        pltpu.SemaphoreType.DMA((len(shapes),)),
        sems(2 * MPS), sems(MPS - 1), sems(2 * MPS - 2), sems(2 * MPS - 2), sems(MPS - 1),
        sems(ROW - 1), sems(MPS - 1), sems(ROW - 1), sems(MPS - 1), sems(ROW - 1),
        sems(2 * MPS), sems(MPS - 1),
        sems(1), sems(XS - 1), sems(FAR - 1), sems(1), sems(XS - 1), sems(FAR - 1),
    ]
    vmem = pl.BlockSpec(memory_space=pltpu.VMEM)
    hbm = pl.BlockSpec(memory_space=pltpu.HBM)
    results = pl.pallas_call(
        body,
        out_shape=shapes,
        in_specs=[hbm] * len(args),
        out_specs=(hbm,) * len(shapes),
        scratch_shapes=scratch,
        compiler_params=pltpu.CompilerParams(
            collective_id=0, has_side_effects=True, vmem_limit_bytes=VMEM_BYTES
        ),
    )(*args)
    return pl.pallas_call(
        write_out,
        out_shape=shapes,
        in_specs=[vmem] * len(shapes),
        out_specs=(vmem,) * len(shapes),
        compiler_params=pltpu.CompilerParams(vmem_limit_bytes=VMEM_BYTES),
    )(*results)


def solution(mesh):
    in_specs = (
        P("mp", "seq"),
        P("mp", "seq"),
        P(None, "mp", None),
        P("mp"),
        P(None, "mp"),
        P("mp"),
        P("seq", "mp"),
        P(None, "mp"),
    )
    out_specs = (P("mp", "seq"), P("mp", "seq"), P("seq", "mp"), P("seq", None, "mp"))
    return jax.shard_map(shards, mesh=mesh, in_specs=in_specs, out_specs=out_specs, check_vma=False)
```
